32 devices in a mesh: visit: 4 (over x, core), patch: 8 (over z, y).
Axes of the slice: x: 2, y: 2, z: 4, core: 2. Of those that a mesh axis runs over, the one named last changes fastest.
Arguments:
- images: bfloat16 [256, 512, 512], P(('visit', 'patch')), may hold values from -10 to 10
- warp_rows: bfloat16 [256, 512, 512], P(('visit', 'patch')), may hold values from -2 to 2
- warp_cols: bfloat16 [256, 512, 512], P(('visit', 'patch')), may hold values from -2 to 2
- tile_weight: bfloat16 [256], P(('visit', 'patch')), may hold values from 0.5 to 4
- tile_patch: int32 [256], P(('visit', 'patch')), may hold values from 0 to 7, as said below
- match_rows: float32 [8, 512, 512], P('patch'), may hold values from -2 to 2
- match_cols: float32 [8, 512, 512], P('patch'), may hold values from -2 to 2
- src_row: int32 [8, 512], P('patch'), may hold values from 0 to 511
- src_col: int32 [8, 512], P('patch'), may hold values from 0 to 511
Outputs:
- coadd: float32 [8, 512, 512], P('patch', 'visit')
- zero_point: float32 [16], P('visit')
- flux_resid: float32 [256, 512], P(('visit', 'patch'))
The draws below stay inside these ranges and needn't reach their ends.
Inputs may be any that keep to these rules, and one draw needn't show every extreme that they name: `tile_patch`: among the 8 tiles of one device no patch is named more than 2 times; in each visit row one patch is named exactly 2 times by every device of the row; every patch is named by some tile of every visit row.
All inputs are finite; a program needn't handle non-finite values.
Results may differ from the reference program's by a relative error of at most 0.0065.
Values may be sent and summed in bfloat16 or wider, within the bound.
No kernel may reach another device: no remote copies, remote signals or barrier semaphores. Data moves between devices by JAX's collectives and lax.ppermute only.
A program may use at most 128 MiB of HBM per device.

```python
import math
import jax
import jax.numpy as jnp
from jax import lax

S = 512
TILES_DEV = 8
VIS_ROW = 4
CAP = 2
SRC = 512
TILES = 256
PATCHES = 8
VISITS = 16
N_VISIT = 4
N_PATCH = 8


def route_table(key):
    devices_all = N_VISIT * N_PATCH
    hot_key, score_key, order_key = jax.random.split(jax.random.fold_in(key, 11), 3)
    hot_patch = jnp.repeat(jax.random.randint(hot_key, (N_VISIT,), 0, N_PATCH), N_PATCH)
    own_patch = jnp.tile(jnp.arange(N_PATCH), N_VISIT)
    places = jnp.arange(2 * N_PATCH)
    candidates = places % N_PATCH
    scores = jax.random.randint(score_key, (devices_all, 2 * N_PATCH), 0, 2 ** 20) * 128 + places[None, :]
    forced = (candidates[None, :] == own_patch[:, None]) & (places[None, :] < N_PATCH)
    scores = jnp.where(forced, scores + 2 ** 28, scores)
    scores = jnp.where(candidates[None, :] == hot_patch[:, None], -2 ** 29, scores)
    ranking = jnp.argsort(-scores, axis=1)
    chosen = candidates[ranking[:, :TILES_DEV - CAP]]
    routes = jnp.concatenate([jnp.repeat(hot_patch[:, None], CAP, axis=1), chosen], axis=1)
    mixing = jax.random.randint(order_key, (devices_all, TILES_DEV), 0, 2 ** 20) * 64 + jnp.arange(TILES_DEV)[None, :]
    routes = jnp.take_along_axis(routes, jnp.argsort(mixing, axis=1), axis=1)
    return routes.reshape(-1).astype(jnp.int32)


def draw_tile_patch(key, part):
    return route_table(key)


def draw_images(key, part):
    routes = route_table(key)
    sky_key, gain_key, noise_key = jax.random.split(jax.random.fold_in(key, 23), 3)
    tile_index = jnp.arange(TILES)
    visit_id = tile_index // (TILES_DEV * N_PATCH) * VIS_ROW + tile_index % TILES_DEV % VIS_ROW
    gains = jnp.exp(jax.random.uniform(gain_key, (VISITS,), minval=-0.7, maxval=0.7))
    sky = jnp.clip(jax.random.normal(sky_key, (N_PATCH, S, S)), -4.0, 4.0)
    noise = 0.5 * jnp.clip(jax.random.normal(noise_key, (TILES, S, S)), -4.0, 4.0)
    return (gains[visit_id][:, None, None] * sky[routes] + noise).astype(jnp.bfloat16)


def near_identity(key, count, spread):
    spread_part = jnp.clip(jax.random.normal(key, (count, S, S)), -4.0, 4.0)
    return jnp.eye(S)[None, :, :] + spread * spread_part / jnp.sqrt(S * 1.0)


def draw_warp_rows(key, part):
    return near_identity(jax.random.fold_in(key, 31), TILES, 0.4).astype(jnp.bfloat16)


def draw_warp_cols(key, part):
    return near_identity(jax.random.fold_in(key, 37), TILES, 0.4).astype(jnp.bfloat16)


def draw_match_rows(key, part):
    return near_identity(jax.random.fold_in(key, 41), PATCHES, 0.3).astype(jnp.float32)


def draw_match_cols(key, part):
    return near_identity(jax.random.fold_in(key, 43), PATCHES, 0.3).astype(jnp.float32)


def with_ends(array, own_key, least, high):
    shape = array.shape
    spot = [jax.random.randint(jax.random.fold_in(own_key, axis), (), 0, shape[axis]) for axis in range(len(shape))]
    array = array.at[tuple(spot)].set(least)
    longest = shape.index(max(shape))
    spot[longest] = (spot[longest] + 1) % shape[longest]
    return array.at[tuple(spot)].set(high)


def level_of(rng, shape, pieces, smallest, high):
    def one(dim, parts):
        draws = jax.random.uniform(jax.random.fold_in(jax.random.fold_in(rng, 6), dim), (parts,), jnp.float32, smallest / len(pieces), high / len(pieces))
        return jnp.repeat(jnp.exp(draws), shape[dim] // parts).reshape((-1,) + (1,) * (len(shape) - dim - 1))

    level = one(*pieces[0])
    for cut in pieces[1:]:
        level = level * one(*cut)
    return level


def setup_inputs(seed: int = 0) -> dict:
    seeds = jax.random.split(jax.random.key(seed), 10)
    images = draw_images(jax.random.fold_in(seeds[9], 71), 0)
    warp_rows = draw_warp_rows(jax.random.fold_in(seeds[9], 71), 0)
    warp_cols = draw_warp_cols(jax.random.fold_in(seeds[9], 71), 0)
    tile_weight = jnp.clip(jnp.exp(math.log(4.0) - 2.0794415 * jax.random.uniform(seeds[3], (TILES,), jnp.float32) ** level_of(seeds[3], (TILES,), ((0, 32),), -0.2, 0.2)), 0.5, 4.0).astype(jnp.bfloat16)
    tile_patch = draw_tile_patch(jax.random.fold_in(seeds[9], 71), 0)
    match_rows = draw_match_rows(jax.random.fold_in(seeds[9], 71), 0)
    match_cols = draw_match_cols(jax.random.fold_in(seeds[9], 71), 0)
    src_row = with_ends(jax.random.randint(seeds[7], (PATCHES, SRC), 0, S), jax.random.fold_in(seeds[7], 1), 0, S - 1).astype(jnp.int32)
    src_col = with_ends(jax.random.randint(seeds[8], (PATCHES, SRC), 0, S), jax.random.fold_in(seeds[8], 1), 0, S - 1).astype(jnp.int32)
    return dict(images=images, warp_rows=warp_rows, warp_cols=warp_cols, tile_weight=tile_weight, tile_patch=tile_patch, match_rows=match_rows, match_cols=match_cols, src_row=src_row, src_col=src_col)


HIGHEST = lax.Precision.HIGHEST
APERTURE = 2.5


def profiles(centers, length):
    pixel_grid = jnp.arange(length).astype(jnp.float32)
    distance = pixel_grid[None, :] - centers.astype(jnp.float32)[:, None]
    return jnp.exp(-distance * distance / (2.0 * APERTURE * APERTURE)).astype(jnp.bfloat16)


def reference(images, warp_rows, warp_cols, tile_weight, tile_patch, match_rows, match_cols, src_row, src_col):
    def warp_one(member):
        detector, row_matrix, col_matrix = member
        half_warp = jnp.dot(detector, col_matrix.T, preferred_element_type=jnp.float32).astype(jnp.bfloat16)
        return jnp.dot(row_matrix, half_warp, preferred_element_type=jnp.float32).astype(jnp.bfloat16)

    warped = lax.map(warp_one, (images, warp_rows, warp_cols))
    weights = tile_weight.astype(jnp.float32)

    def add_tile(running, member):
        tile_data, weight, patch_id = member
        return running.at[patch_id].add(weight * tile_data.astype(jnp.float32)), None

    stacked, _ = lax.scan(add_tile, jnp.zeros((PATCHES, S, S), jnp.float32), (warped, weights, tile_patch))
    total_weight = jax.ops.segment_sum(weights, tile_patch, PATCHES)
    matched = jnp.einsum('pij,pjk->pik', match_rows, stacked, precision=HIGHEST)
    matched = jnp.einsum('pik,plk->pil', matched, match_cols, precision=HIGHEST)
    coadd = matched / total_weight[:, None, None]
    row_prof = jax.vmap(lambda centers: profiles(centers, S))(src_row)
    col_prof = jax.vmap(lambda centers: profiles(centers, S))(src_col)
    by_column = jnp.einsum('pyx,pqx->pyq', coadd, col_prof.astype(jnp.float32), precision=HIGHEST)
    ref_flux = jnp.einsum('pyq,pqy->pq', by_column, row_prof.astype(jnp.float32), precision=HIGHEST)

    def measure(member):
        tile_data, patch_id = member
        tile_cols = jnp.dot(tile_data, col_prof[patch_id].T, preferred_element_type=jnp.float32)
        return jnp.einsum('yq,qy->q', tile_cols, row_prof[patch_id].astype(jnp.float32), precision=HIGHEST)

    fluxes = lax.map(measure, (warped, tile_patch))
    tile_ref = ref_flux[tile_patch]
    tile_index = jnp.arange(TILES)
    visit_id = (tile_index // (TILES_DEV * N_PATCH)) * VIS_ROW + (tile_index % TILES_DEV) % VIS_ROW
    numerator = jax.ops.segment_sum(jnp.sum(fluxes * tile_ref, axis=1), visit_id, VISITS)
    denominator = jax.ops.segment_sum(jnp.sum(tile_ref * tile_ref, axis=1), visit_id, VISITS)
    zero_point = numerator / denominator
    flux_resid = fluxes - zero_point[visit_id][:, None] * tile_ref
    return coadd, zero_point, flux_resid
```

```python
import functools

import jax
import jax.numpy as jnp
from jax import lax
from jax.experimental import pallas as pl
from jax.experimental.pallas import tpu as pltpu
from jax.sharding import PartitionSpec as P

VIS_ROW = 4
APERTURE = 2.5
HIGHEST = lax.Precision.HIGHEST
F32 = jnp.float32
BF16 = jnp.bfloat16
AXES = ("visit", "patch")
EXPONENT = -1.4426950408889634 / (2.0 * APERTURE * APERTURE)
VMEM_LIMIT = 56 * 1024 * 1024
NT = (((1,), (1,)), ((), ()))
TN = (((0,), (0,)), ((), ()))


class Layout:
    def __init__(self, tiles, side):
        self.tiles, self.side = tiles, side
        self.visits, self.patches = lax.axis_size("visit"), lax.axis_size("patch")
        self.group = self.visits // 2
        self.highs = self.patches // self.group
        self.width = side // self.visits
        self.part = self.width // 2
        self.rows = self.part * self.visits

    def place(self):
        visit, patch = lax.axis_index("visit"), lax.axis_index("patch")
        return visit % 2, visit // 2, patch // self.group, patch % self.group

    def permute(self, array, partner):
        pairs = []
        for visit in range(self.visits):
            for patch in range(self.patches):
                x, core, high, low = partner(visit // 2, visit % 2, patch // self.group, patch % self.group)
                target = (2 * x + core) * self.patches + self.group * high + low
                pairs.append((visit * self.patches + patch, target))
        return lax.ppermute(array, AXES, pairs)

    def swap_core(self, array):
        return self.permute(array, lambda x, core, high, low: (x, 1 - core, high, low))

    def swap_first(self, array, step):
        def partner(x, core, high, low):
            return (x ^ step, core, high, low) if core == 0 else (x, core, high, low ^ step)

        return self.permute(array, partner)

    def swap_second(self, array, step):
        def partner(x, core, high, low):
            return (x, core, high, low ^ step) if core == 0 else (x ^ step, core, high, low)

        return self.permute(array, partner)

    def swap_low(self, array, step):
        return self.permute(array, lambda x, core, high, low: (x, core, high, low ^ step))

    def swap_high(self, array, step):
        return self.permute(array, lambda x, core, high, low: (x, core, high ^ step, low))

    def swap_visit(self, array, step):
        def partner(x, core, high, low):
            visit = (2 * x + core) ^ step
            return visit // 2, visit % 2, high, low

        return self.permute(array, partner)


def warp_kernel(lay, patch_ref, weight_ref, image, rows, cols, warped, send, keep, total):
    tile = pl.program_id(0)

    @pl.when(tile == 0)
    def _():
        total[...] = jnp.zeros_like(total)

    cols_part = cols[0].reshape(lay.rows, lay.side)
    half = lax.dot_general(cols_part, image[0], NT, preferred_element_type=F32).astype(BF16)
    result = lax.dot_general(half, rows[0], NT, preferred_element_type=F32).astype(BF16)
    warped[0] = result
    total[patch_ref[tile]] += weight_ref[tile] * result.astype(F32)

    @pl.when(tile == lay.tiles - 1)
    def _():
        core = lax.axis_index("visit") % 2
        for out, own in ((send, 1 - core), (keep, core)):
            for first in range(lay.group):
                for second in range(lay.group):
                    x = jnp.where(own == 0, first, second)
                    low = jnp.where(own == 0, second, first)
                    start = pl.multiple_of((2 * x + own) * lay.part, lay.part)
                    for high in range(lay.highs):
                        block = total[high * lay.group + low, pl.ds(start, lay.part), :]
                        out[first, second, high] = block.astype(BF16)


def warp(lay, part, tile_patch, weight, images, warp_rows, cols):
    tiles, side = lay.tiles, lay.side
    pieces = (lay.group, lay.group, lay.highs, lay.part, side)
    whole = lambda tile, *_: (0, 0, 0, 0, 0)
    return pl.pallas_call(
        functools.partial(warp_kernel, lay),
        grid_spec=pltpu.PrefetchScalarGridSpec(
            num_scalar_prefetch=2,
            grid=(tiles,),
            in_specs=[
                pl.BlockSpec((1, side, side), lambda tile, *_: (tile, 0, 0)),
                pl.BlockSpec((1, side, side), lambda tile, *_: (tile, 0, 0)),
                pl.BlockSpec((1, lay.visits, None, lay.part, side), lambda tile, *_: (tile, 0, part, 0, 0)),
            ],
            out_specs=[
                pl.BlockSpec((1, lay.rows, side), lambda tile, *_: (tile, 0, 0)),
                pl.BlockSpec(pieces, whole),
                pl.BlockSpec(pieces, whole),
            ],
            scratch_shapes=[pltpu.VMEM((lay.patches, lay.rows, side), F32)],
        ),
        out_shape=[
            jax.ShapeDtypeStruct((tiles, lay.rows, side), BF16),
            jax.ShapeDtypeStruct(pieces, BF16),
            jax.ShapeDtypeStruct(pieces, BF16),
        ],
        compiler_params=pltpu.CompilerParams(vmem_limit_bytes=VMEM_LIMIT),
        cost_estimate=pl.CostEstimate(
            flops=4 * tiles * lay.rows * side * side, bytes_accessed=6 * tiles * side * side, transcendentals=0
        ),
        name="warp",
    )(tile_patch, weight, images, warp_rows, cols)


def profile(position, centers):
    distance = position - centers
    return jnp.exp2(distance * distance * EXPONENT).astype(BF16)


def flux_kernel(lay, patch_ref, place_ref, warped_a, warped_b, src_row, src_col, flux, sums):
    tile = pl.program_id(0)
    side = lay.side

    @pl.when(tile == 0)
    def _():
        sums[...] = jnp.zeros_like(sums)

    row_prof = profile(lax.broadcasted_iota(jnp.int32, (side, side), 0).astype(F32), src_row[0])
    local = lax.broadcasted_iota(jnp.int32, (lay.rows, side), 0)
    value = jnp.zeros((1, side), F32)
    for part, warped in enumerate((warped_a, warped_b)):
        by_row = jnp.dot(warped[0], row_prof, preferred_element_type=F32)
        column = (local // lay.part) * lay.width + part * lay.part + local % lay.part
        col_prof = profile(column.astype(F32), src_col[0])
        value += jnp.sum(by_row * col_prof.astype(F32), axis=0, keepdims=True)
    flux[0] = value
    spot = (tile % VIS_ROW) * lay.patches + patch_ref[tile]
    sums[pl.ds(spot, 1), :] += value


def forced_flux(lay, tile_patch, tile_place, warped_a, warped_b, src_row, src_col):
    tiles, side = lay.tiles, lay.side
    return pl.pallas_call(
        functools.partial(flux_kernel, lay),
        grid_spec=pltpu.PrefetchScalarGridSpec(
            num_scalar_prefetch=2,
            grid=(tiles,),
            in_specs=[
                pl.BlockSpec((1, lay.rows, side), lambda tile, *_: (tile, 0, 0)),
                pl.BlockSpec((1, lay.rows, side), lambda tile, *_: (tile, 0, 0)),
                pl.BlockSpec((1, 1, side), lambda tile, patch, place: (place[tile], 0, 0)),
                pl.BlockSpec((1, 1, side), lambda tile, patch, place: (place[tile], 0, 0)),
            ],
            out_specs=[
                pl.BlockSpec((1, 1, side), lambda tile, *_: (tile, 0, 0)),
                pl.BlockSpec((VIS_ROW * lay.patches, side), lambda tile, *_: (0, 0)),
            ],
        ),
        out_shape=[
            jax.ShapeDtypeStruct((tiles, 1, side), F32),
            jax.ShapeDtypeStruct((VIS_ROW * lay.patches, side), F32),
        ],
        compiler_params=pltpu.CompilerParams(vmem_limit_bytes=VMEM_LIMIT),
        cost_estimate=pl.CostEstimate(
            flops=2 * tiles * side**3, bytes_accessed=2 * tiles * side * side, transcendentals=2 * tiles * side * side
        ),
        name="forced_flux",
    )(tile_patch, tile_place, warped_a, warped_b, src_row, src_col)


def prepare_kernel(lay, src_row, src_col, match_cols, row_prof, col_match):
    position = lax.broadcasted_iota(jnp.int32, (lay.side, lay.side), 0).astype(F32)
    row_prof[...] = profile(position, src_row[...])
    col_prof = profile(position, src_col[...]).astype(F32)
    product = lax.dot_general(match_cols[...], col_prof, TN, precision=HIGHEST, preferred_element_type=F32)
    col_match[...] = product.reshape(lay.visits, lay.width, lay.side)


def prepare(lay, src_row, src_col, match_cols):
    side = lay.side
    return pl.pallas_call(
        functools.partial(prepare_kernel, lay),
        out_shape=[
            jax.ShapeDtypeStruct((side, side), BF16),
            jax.ShapeDtypeStruct((lay.visits, lay.width, side), F32),
        ],
        compiler_params=pltpu.CompilerParams(vmem_limit_bytes=VMEM_LIMIT),
        cost_estimate=pl.CostEstimate(
            flops=12 * side**3, bytes_accessed=10 * side * side, transcendentals=2 * side * side
        ),
        name="prepare",
    )(src_row, src_col, match_cols)


def match_kernel(lay, extra, stacked_a, stacked_b, match_rows, row_prof, col_match, weight, message):
    side, width = lay.side, lay.width
    visit = lax.axis_index("visit")
    stacked = jnp.concatenate([stacked_a[...], stacked_b[...]], axis=0)
    matched = lax.dot_general(match_rows[...], stacked, NT, precision=HIGHEST, preferred_element_type=F32)
    by_row = lax.dot_general(
        matched.T, row_prof[...].astype(F32), (((1,), (0,)), ((), ())), precision=HIGHEST, preferred_element_type=F32
    )
    flux = jnp.sum(by_row * col_match[visit], axis=0, keepdims=True)
    tail = jnp.concatenate(
        [flux[:, block * width : (block + 1) * width] for block in range(lay.visits)]
        + [jnp.broadcast_to(weight[...], (extra - lay.visits, width))],
        axis=0,
    )
    for block in range(lay.visits):
        message[block, :width] = matched[block * width : (block + 1) * width]
        message[block, width:] = tail


def match(lay, extra, stacked_a, stacked_b, match_rows, row_prof, col_match, weight):
    side, width = lay.side, lay.width
    return pl.pallas_call(
        functools.partial(match_kernel, lay, extra),
        out_shape=jax.ShapeDtypeStruct((lay.visits, width + extra, width), F32),
        compiler_params=pltpu.CompilerParams(vmem_limit_bytes=VMEM_LIMIT),
        cost_estimate=pl.CostEstimate(
            flops=24 * width * side * side, bytes_accessed=8 * side * side, transcendentals=0
        ),
        name="match",
    )(stacked_a, stacked_b, match_rows, row_prof, col_match, weight)


def finish_kernel(lay, patch_ref, counts, flux, sums, *refs):
    messages, zero, resid, table = refs[: lay.highs], refs[-3], refs[-2], refs[-1]
    patch = lax.axis_index("patch")
    high, low = patch // lay.group, patch % lay.group
    for step_high in range(lay.highs):
        for step_low in range(lay.group):
            data = messages[step_high][step_low]
            rows = data[: lay.visits] / data[lay.visits : lay.visits + 1]
            spot = (high ^ step_high) * lay.group + (low ^ step_low)
            line = jnp.concatenate([rows[block : block + 1] for block in range(lay.visits)], axis=1)
            table[pl.ds(spot, 1), :] = line
    reference = table[...]
    squares = jnp.sum(reference * reference, axis=1, keepdims=True)
    scales = []
    for visit in range(VIS_ROW):
        numerator = jnp.sum(sums[visit * lay.patches : (visit + 1) * lay.patches] * reference, keepdims=True)
        denominator = jnp.sum(counts[visit * lay.patches : (visit + 1) * lay.patches] * squares, keepdims=True)
        scales.append(numerator / denominator)
        zero[visit : visit + 1, :] = jnp.broadcast_to(scales[-1], (1, zero.shape[1]))
    for tile in range(lay.tiles):
        own = table[pl.ds(patch_ref[tile], 1), :]
        resid[tile : tile + 1, :] = flux[tile] - scales[tile % VIS_ROW] * own


def finish(lay, tile_patch, counts, flux, sums, messages):
    vmem = pl.BlockSpec(memory_space=pltpu.VMEM)
    return pl.pallas_call(
        functools.partial(finish_kernel, lay),
        in_specs=[pl.BlockSpec(memory_space=pltpu.SMEM)] + [vmem] * (3 + len(messages)),
        out_specs=[vmem, vmem],
        out_shape=[
            jax.ShapeDtypeStruct((VIS_ROW, 128), F32),
            jax.ShapeDtypeStruct((lay.tiles, lay.side), F32),
        ],
        scratch_shapes=[pltpu.VMEM((lay.patches, lay.side), F32)],
        name="finish",
    )(tile_patch, counts, flux, sums, *messages)


def pick(array, index):
    return lax.dynamic_index_in_dim(array, index, 0, keepdims=False).astype(F32)


def scatter_sum(lay, send, keep):
    core, x, high, low = lay.place()
    first = jnp.where(core == 0, x, low)
    second = jnp.where(core == 0, low, x)
    terms = [keep, lay.swap_core(send)]
    for index, size, swap in (
        (first, lay.group, lay.swap_first),
        (second, lay.group, lay.swap_second),
        (high, lay.highs, lay.swap_high),
    ):
        received = []
        for step in range(1, size):
            outgoing = sum(pick(term, index ^ step) for term in terms).astype(BF16)
            received.append(swap(outgoing, step))
        terms = [sum(pick(term, index) for term in terms)] + received
    return sum(term.astype(F32) for term in terms)


def gather_patch(lay, array):
    near = jnp.stack([array] + [lay.swap_low(array, step) for step in range(1, lay.group)])
    return [near] + [lay.swap_high(near, step) for step in range(1, lay.highs)]


def sum_patch(lay, array):
    array = sum([lay.swap_low(array, step) for step in range(1, lay.group)], array)
    return sum([lay.swap_high(array, step) for step in range(1, lay.highs)], array)


def shards(
    images, warp_rows, warp_cols, tile_weight, tile_patch, match_rows, match_cols, src_row, src_col
):
    lay = Layout(images.shape[0], images.shape[1])
    tiles, side = lay.tiles, lay.side
    core, x, high, low = lay.place()
    visit, patch = lax.axis_index("visit"), lax.axis_index("patch")
    weight = tile_weight.astype(F32)
    cols = warp_cols.reshape(tiles, lay.visits, 2, lay.part, side)

    warped_a, send_a, keep_a = warp(lay, 0, tile_patch, weight, images, warp_rows, cols)
    warped_b, send_b, keep_b = warp(lay, 1, tile_patch, weight, images, warp_rows, cols)

    named = (tile_patch[:, None] == jnp.arange(lay.patches)[None, :]).astype(F32)
    local_counts = jnp.sum(named.reshape(tiles // VIS_ROW, VIS_ROW, lay.patches), axis=0).reshape(-1)
    local_weight = jnp.sum(named * weight[:, None], axis=0)
    extras = jnp.concatenate([local_counts, local_weight])
    extras = jnp.pad(extras, (0, side - extras.shape[0]))
    sources = jnp.stack([src_row[0].astype(F32), src_col[0].astype(F32), extras])
    gathered = jnp.stack(gather_patch(lay, sources)).reshape(lay.patches, 3, side)
    all_rows, all_cols = gathered[:, 0:1, :], gathered[:, 1:2, :]
    extras = jnp.sum(gathered[:, 2, :], axis=0)
    counts = extras[: VIS_ROW * lay.patches].reshape(VIS_ROW * lay.patches, 1)
    weight_part = lax.dynamic_slice_in_dim(extras, VIS_ROW * lay.patches + patch, 1, 0).reshape(1, 1)
    tile_place = ((tile_patch // lay.group) ^ high) * lay.group + ((tile_patch % lay.group) ^ low)

    stacked_a = scatter_sum(lay, send_a, keep_a)
    stacked_b = scatter_sum(lay, send_b, keep_b)

    flux, sums = forced_flux(lay, tile_patch, tile_place, warped_a, warped_b, all_rows, all_cols)
    sums = sum_patch(lay, sums)
    row_prof, col_match = prepare(lay, src_row.astype(F32), src_col.astype(F32), match_cols[0])

    extra = -(-(lay.visits + 1) // 8) * 8
    width = lay.width
    message = match(lay, extra, stacked_a, stacked_b, match_rows[0], row_prof, col_match, weight_part)
    parts = [pick(message, visit)]
    parts += [lay.swap_visit(pick(message, visit ^ step), step) for step in range(1, lay.visits)]
    reference = sum(part[width:] for part in parts)
    messages = gather_patch(lay, reference)

    by_visit = match_cols[0].reshape(side, lay.visits, width).transpose(1, 0, 2)
    coadd = sum(
        lax.dot_general(
            part[:width],
            lax.dynamic_index_in_dim(by_visit, visit ^ step, 0, keepdims=False),
            NT,
            precision=HIGHEST,
            preferred_element_type=F32,
        )
        for step, part in enumerate(parts)
    )
    coadd = coadd / reference[lay.visits, 0]

    zero, resid = finish(lay, tile_patch, counts, flux, sums, messages)
    return (coadd[None], zero[:, 0], resid)


def solution(mesh):
    in_specs = (
        P(AXES, None, None),
        P(AXES, None, None),
        P(AXES, None, None),
        P(AXES),
        P(AXES),
        P("patch", None, None),
        P("patch", None, None),
        P("patch", None),
        P("patch", None),
    )
    out_specs = (P("patch", "visit", None), P("visit"), P(AXES, None))
    return jax.shard_map(shards, mesh=mesh, in_specs=in_specs, out_specs=out_specs, check_vma=False)
```

```python
import functools

import jax
import jax.numpy as jnp
from jax import lax
from jax.experimental import pallas as pl
from jax.experimental.pallas import tpu as pltpu
from jax.sharding import PartitionSpec as P

VIS_ROW = 4
APERTURE = 2.5
HIGHEST = lax.Precision.HIGHEST
F32 = jnp.float32
BF16 = jnp.bfloat16
AXES = ("visit", "patch")
EXPONENT = -1.4426950408889634 / (2.0 * APERTURE * APERTURE)
VMEM_LIMIT = 20 * 1024 * 1024
WARP_LIMIT = 38 * 1024 * 1024
PARTS = 1
PAIR = 2
IN_VMEM = pl.BlockSpec(memory_space=pltpu.VMEM)
NT = (((1,), (1,)), ((), ()))
TN = (((0,), (0,)), ((), ()))


class Layout:
    def __init__(self, tiles, side):
        self.tiles, self.side = tiles, side
        self.visits, self.patches = lax.axis_size("visit"), lax.axis_size("patch")
        self.group = self.visits // 2
        self.highs = self.patches // self.group
        self.width = side // self.visits
        self.part = side // PARTS

    def place(self):
        visit, patch = lax.axis_index("visit"), lax.axis_index("patch")
        return visit % 2, visit // 2, patch // self.group, patch % self.group

    def permute(self, array, partner):
        pairs = []
        for visit in range(self.visits):
            for patch in range(self.patches):
                x, core, high, low = partner(visit // 2, visit % 2, patch // self.group, patch % self.group)
                target = (2 * x + core) * self.patches + self.group * high + low
                pairs.append((visit * self.patches + patch, target))
        return lax.ppermute(array, AXES, pairs)

    def swap_core(self, array):
        return self.permute(array, lambda x, core, high, low: (x, 1 - core, high, low))

    def swap_first(self, array, step):
        def partner(x, core, high, low):
            return (x ^ step, core, high, low) if core == 0 else (x, core, high, low ^ step)

        return self.permute(array, partner)

    def swap_second(self, array, step):
        def partner(x, core, high, low):
            return (x, core, high, low ^ step) if core == 0 else (x ^ step, core, high, low)

        return self.permute(array, partner)

    def swap_low(self, array, step):
        return self.permute(array, lambda x, core, high, low: (x, core, high, low ^ step))

    def swap_high(self, array, step):
        return self.permute(array, lambda x, core, high, low: (x, core, high ^ step, low))

    def swap_visit(self, array, step):
        def partner(x, core, high, low):
            visit = (2 * x + core) ^ step
            return visit // 2, visit % 2, high, low

        return self.permute(array, partner)


def warp_kernel(lay, patch_ref, weight_ref, images, rows, cols, warped, *refs):
    outs, (image, row, col, half, result, weights, total, arrive, leave, small) = refs[: 2 * PARTS], refs[2 * PARTS :]
    sends, keeps = outs[:PARTS], outs[PARTS:]
    fetch = pltpu.make_async_copy(weight_ref, weights, small)
    fetch.start()
    loads = []
    for tile in range(lay.tiles):
        loads.append(
            [
                pltpu.make_async_copy(source.at[tile], target.at[tile], arrive.at[kind, tile])
                for kind, (source, target) in enumerate(((images, image), (cols, col), (rows, row)))
            ]
        )
        for load in loads[-1]:
            load.start()
    total[...] = jnp.zeros_like(total)
    fetch.wait()
    lane = lax.broadcasted_iota(jnp.int32, (1, lay.tiles), 1)
    stores = []
    for tile in range(lay.tiles + 1):
        if tile < lay.tiles:
            loads[tile][0].wait()
            loads[tile][1].wait()
            half[tile % 2] = lax.dot_general(image[tile], col[tile], NT, preferred_element_type=F32).astype(BF16)
        if tile:
            last = tile - 1
            loads[last][2].wait()
            value = jnp.dot(row[last], half[last % 2], preferred_element_type=F32).astype(BF16)
            result[last] = value
            stores.append(pltpu.make_async_copy(result.at[last], warped.at[last], leave.at[last]))
            stores[-1].start()
            spread = weights[...].astype(F32).reshape(1, lay.tiles)
            weight = jnp.sum(jnp.where(lane == last, spread, 0.0), keepdims=True)
            total[patch_ref[last]] += weight * value.astype(F32)

    def write(outs, core):
        for first in range(lay.group):
            for second in range(lay.group):
                x, low = (first, second) if core == 0 else (second, first)
                start = (2 * x + core) * lay.width
                for high in range(lay.highs):
                    for part, out in enumerate(outs):
                        block = total[
                            high * lay.group + low,
                            part * lay.part : (part + 1) * lay.part,
                            start : start + lay.width,
                        ]
                        out[first, second, high] = block.astype(BF16)

    core = lax.axis_index("visit") % 2
    for own in range(2):

        @pl.when(core == own)
        def _():
            write(sends, 1 - own)
            write(keeps, own)

    for store in stores:
        store.wait()


def in_hbm(array):
    return pltpu.with_memory_space_constraint(array, pltpu.HBM)


def warp(lay, tile_patch, weight, images, warp_rows, warp_cols):
    tiles, side = lay.tiles, lay.side
    pieces = (lay.group, lay.group, lay.highs, lay.part, lay.width)
    in_any = pl.BlockSpec(memory_space=pltpu.HBM)
    stack = pltpu.VMEM((tiles, side, side), BF16)
    out = pl.pallas_call(
        functools.partial(warp_kernel, lay),
        in_specs=[pl.BlockSpec(memory_space=pltpu.SMEM)] + [in_any] * 4,
        out_specs=[in_any] + [IN_VMEM] * (2 * PARTS),
        out_shape=[pltpu.HBM((tiles, side, side), BF16)] + [pltpu.VMEM(pieces, BF16)] * (2 * PARTS),
        scratch_shapes=[
            stack,
            stack,
            stack,
            pltpu.VMEM((2, side, side), BF16),
            stack,
            pltpu.VMEM((tiles,), BF16),
            pltpu.VMEM((lay.patches, side, side), F32),
            pltpu.SemaphoreType.DMA((3, tiles)),
            pltpu.SemaphoreType.DMA((tiles,)),
            pltpu.SemaphoreType.DMA,
        ],
        compiler_params=pltpu.CompilerParams(vmem_limit_bytes=WARP_LIMIT),
        cost_estimate=pl.CostEstimate(
            flops=4 * tiles * side**3, bytes_accessed=8 * tiles * side * side, transcendentals=0
        ),
        name="warp",
    )(tile_patch, weight, images, warp_rows, warp_cols)
    return out[0], out[1 : 1 + PARTS], out[1 + PARTS :]


def profile(position, centers):
    distance = position - centers
    return jnp.exp2(distance * distance * EXPONENT).astype(BF16)


def flux_kernel(lay, patch_ref, place_ref, warped, *refs):
    step = pl.program_id(0)
    sources, (flux, sums) = refs[: 2 * PAIR], refs[2 * PAIR :]

    @pl.when(step == 0)
    def _():
        sums[...] = jnp.zeros_like(sums)

    position = lax.broadcasted_iota(jnp.int32, (lay.side, lay.side), 0).astype(F32)
    for local in range(PAIR):
        tile = step * PAIR + local
        row_prof = profile(position, sources[local][0])
        col_prof = profile(position, sources[PAIR + local][0])
        by_column = jnp.dot(warped[local], col_prof, preferred_element_type=F32)
        value = jnp.sum(by_column * row_prof.astype(F32), axis=0, keepdims=True)
        flux[tile] = value
        spot = patch_ref[tile] * VIS_ROW + tile % VIS_ROW
        sums[pl.ds(spot, 1), :] += value


def forced_flux(lay, tile_patch, tile_place, warped, src_row, src_col):
    tiles, side = lay.tiles, lay.side
    sources = [
        pl.BlockSpec((1, 1, side), lambda step, patch, place, local=local: (place[step * PAIR + local], 0, 0))
        for local in range(PAIR)
    ]
    return pl.pallas_call(
        functools.partial(flux_kernel, lay),
        grid_spec=pltpu.PrefetchScalarGridSpec(
            num_scalar_prefetch=2,
            grid=(tiles // PAIR,),
            in_specs=[pl.BlockSpec((PAIR, side, side), lambda step, *_: (step, 0, 0))] + sources * 2,
            out_specs=[IN_VMEM, IN_VMEM],
        ),
        out_shape=[
            jax.ShapeDtypeStruct((tiles, 1, side), F32),
            jax.ShapeDtypeStruct((VIS_ROW * lay.patches, side), F32),
        ],
        compiler_params=pltpu.CompilerParams(vmem_limit_bytes=VMEM_LIMIT),
        cost_estimate=pl.CostEstimate(
            flops=2 * tiles * side**3, bytes_accessed=2 * tiles * side * side, transcendentals=2 * tiles * side * side
        ),
        name="forced_flux",
    )(tile_patch, tile_place, in_hbm(warped), *([src_row] * PAIR + [src_col] * PAIR))


def split(array):
    upper = array.astype(BF16)
    return upper, (array - upper.astype(F32)).astype(BF16)


def dot3(left, right, dims):
    product = functools.partial(lax.dot_general, dimension_numbers=dims, preferred_element_type=F32)
    return product(left[0], right[0]) + (product(left[0], right[1]) + product(left[1], right[0]))


def prepare_kernel(lay, src_row, src_col, match_rows, match_cols, rows_up, rows_low, row_flux, col_up, col_low, product_ref):
    side = lay.side
    product = functools.partial(lax.dot_general, dimension_numbers=TN, preferred_element_type=F32)
    position = lax.broadcasted_iota(jnp.int32, (side, side), 0).astype(F32)
    row_prof = profile(position, src_row[...].astype(F32))
    col_prof = profile(position, src_col[...].astype(F32))
    upper, lower = split(match_rows[...])
    rows_up[...], rows_low[...] = upper, lower
    row_flux[...] = product(upper, row_prof) + product(lower, row_prof)
    upper, lower = split(match_cols[...])
    product_ref[...] = (product(upper, col_prof) + product(lower, col_prof)).reshape(lay.visits, lay.width, side)
    col_up[...], col_low[...] = split(product_ref[lax.axis_index("visit")])


def prepare(lay, src_row, src_col, match_rows, match_cols):
    side = lay.side
    block = pltpu.HBM((lay.width, side), BF16)
    square = pltpu.HBM((side, side), BF16)
    return pl.pallas_call(
        functools.partial(prepare_kernel, lay),
        in_specs=[IN_VMEM] * 4,
        out_shape=[square, square, pltpu.HBM((side, side), F32), block, block],
        scratch_shapes=[pltpu.VMEM((lay.visits, lay.width, side), F32)],
        compiler_params=pltpu.CompilerParams(vmem_limit_bytes=VMEM_LIMIT),
        cost_estimate=pl.CostEstimate(
            flops=8 * side**3, bytes_accessed=20 * side * side, transcendentals=2 * side * side
        ),
        name="prepare",
    )(src_row, src_col, match_rows, match_cols)


def match_kernel(lay, extra, *refs):
    width, visits = lay.width, lay.visits
    pieces, refs = refs[: PARTS * lay.highs], refs[PARTS * lay.highs :]
    (rows_up, rows_low, row_flux, col_up, col_low, table), refs = refs[:6], refs[6:]
    messages, (spread, matched) = refs[:visits], refs[visits:]
    visit, patch = lax.axis_index("visit"), lax.axis_index("patch")
    stacked = jnp.concatenate(
        [
            sum(piece[...].astype(F32) for piece in pieces[part * lay.highs : (part + 1) * lay.highs])
            for part in range(PARTS)
        ],
        axis=0,
    )
    stacked = split(stacked)
    nn = (((1,), (0,)), ((), ()))
    result = dot3((rows_up[...], rows_low[...]), stacked, nn)
    matched[...] = result.reshape(visits, width, width)
    by_source = dot3(stacked, (col_up[...], col_low[...]), nn)
    flux = jnp.sum(by_source * row_flux[...], axis=0, keepdims=True)
    lane = lax.broadcasted_iota(jnp.int32, table.shape, 1)
    weight = jnp.sum(jnp.where(lane == patch * 8 + VIS_ROW, table[...], 0.0), keepdims=True)
    tail = jnp.concatenate(
        [flux[:, block * width : (block + 1) * width] for block in range(visits)]
        + [jnp.broadcast_to(weight, (extra - visits, width))],
        axis=0,
    )
    spread[...] = jnp.broadcast_to(tail[None], spread.shape)
    upper, lower = split(jnp.broadcast_to(weight, (8, width)))
    weight = jnp.concatenate([upper, lower], axis=0)
    for step, message in enumerate(messages):
        message[:width] = matched[visit ^ step].astype(BF16)
        message[width:] = weight


def match(lay, extra, pieces, prepared, table):
    side, width = lay.side, lay.width
    out = pl.pallas_call(
        functools.partial(match_kernel, lay, extra),
        in_specs=[IN_VMEM] * (len(pieces) + len(prepared) + 1),
        out_specs=[IN_VMEM] * (lay.visits + 1),
        out_shape=[pltpu.VMEM((width + 16, width), BF16)] * lay.visits
        + [jax.ShapeDtypeStruct((lay.visits * lay.patches, extra, width), F32)],
        scratch_shapes=[pltpu.VMEM((lay.visits, width, width), F32)],
        compiler_params=pltpu.CompilerParams(vmem_limit_bytes=VMEM_LIMIT),
        cost_estimate=pl.CostEstimate(
            flops=12 * width * side * side, bytes_accessed=10 * side * side, transcendentals=0
        ),
        name="match",
    )(*pieces, *prepared, table)
    return out[: lay.visits], out[lay.visits]


def coadd_kernel(lay, match_cols, *refs):
    parts, coadd = refs[:-1], refs[-1]
    width = lay.width
    visit = lax.axis_index("visit")
    blocks = []
    for block in range(lay.visits):
        value = parts[0][:width]
        for step in range(1, lay.visits):
            value = jnp.where((visit ^ step) == block, parts[step][:width], value)
        blocks.append(value)
    weight = 0.0
    for part in parts:
        halves = part[width:].astype(F32)
        weight = weight + (halves[0:1, 0:1] + halves[8:9, 0:1])
    blocks = jnp.concatenate(blocks, axis=1)
    product = functools.partial(lax.dot_general, dimension_numbers=NT, preferred_element_type=F32)
    upper, lower = split(match_cols[...])
    product = product(blocks, upper) + product(blocks, lower)
    coadd[...] = product / weight


def coadd_rows(lay, match_cols, parts):
    side, width = lay.side, lay.width
    return pl.pallas_call(
        functools.partial(coadd_kernel, lay),
        out_shape=jax.ShapeDtypeStruct((width, side), F32),
        compiler_params=pltpu.CompilerParams(vmem_limit_bytes=VMEM_LIMIT),
        cost_estimate=pl.CostEstimate(
            flops=12 * width * side * side, bytes_accessed=6 * side * side, transcendentals=0
        ),
        name="coadd_rows",
    )(match_cols, *parts)


def finish_kernel(lay, patch_ref, table, flux, sums, messages, zero, resid, lines):
    visits, patches = lay.visits, lay.patches
    for patch in range(patches):
        data = sum(messages[visit * patches + patch] for visit in range(visits))
        data = data / data[visits : visits + 1]
        lines[patch : patch + 1, :] = jnp.concatenate([data[block : block + 1] for block in range(visits)], axis=1)
    reference = lines[...]
    lane = lax.broadcasted_iota(jnp.int32, (patches, lay.side), 1) // 8
    row = lax.broadcasted_iota(jnp.int32, (patches, lay.side), 0)
    squares = jnp.sum(reference * reference, axis=1, keepdims=True)
    chosen = jnp.sum(jnp.where(lane == row, squares, 0.0), axis=0, keepdims=True) * table[...]
    products = 0.0
    denominators = 0.0
    for patch in range(patches):
        products = products + sums[patch] * reference[patch : patch + 1]
        denominators = denominators + chosen[:, patch * 8 : (patch + 1) * 8]
    columns = jnp.sum(products, axis=1, keepdims=True)
    place = lax.broadcasted_iota(jnp.int32, (1, VIS_ROW), 1)
    numerators = sum(jnp.where(place == visit, columns[visit : visit + 1], 0.0) for visit in range(VIS_ROW))
    scales = numerators / denominators[:, :VIS_ROW]
    zero[...] = scales
    for tile in range(lay.tiles):
        own = lines[pl.ds(patch_ref[tile], 1), :]
        visit = tile % VIS_ROW
        resid[tile : tile + 1, :] = flux[tile] - scales[:, visit : visit + 1] * own


def finish(lay, tile_patch, table, flux, sums, messages):
    return pl.pallas_call(
        functools.partial(finish_kernel, lay),
        in_specs=[pl.BlockSpec(memory_space=pltpu.SMEM)] + [IN_VMEM] * 4,
        out_specs=[IN_VMEM, IN_VMEM],
        out_shape=[
            jax.ShapeDtypeStruct((1, VIS_ROW), F32),
            jax.ShapeDtypeStruct((lay.tiles, lay.side), F32),
        ],
        scratch_shapes=[pltpu.VMEM((lay.patches, lay.side), F32)],
        compiler_params=pltpu.CompilerParams(vmem_limit_bytes=VMEM_LIMIT),
        name="finish",
    )(tile_patch, table, flux, sums, messages)


def spread_kernel(count, place_ref, kept, received, own, *sends):
    for step, out in enumerate((own, *sends)):
        spot = place_ref[0] ^ step
        out[...] = (kept[spot].astype(F32) + received[spot].astype(F32)).astype(out.dtype)


def spread(place, terms):
    kept, received = terms
    count, shape = kept.shape[0], kept.shape[1:]
    out = pl.pallas_call(
        functools.partial(spread_kernel, count),
        in_specs=[pl.BlockSpec(memory_space=pltpu.SMEM), IN_VMEM, IN_VMEM],
        out_specs=[IN_VMEM] * count,
        out_shape=[pltpu.VMEM(shape, BF16)] * count,
        compiler_params=pltpu.CompilerParams(vmem_limit_bytes=VMEM_LIMIT),
        name="spread",
    )(place.reshape(1).astype(jnp.int32), kept, received)
    return out[0], out[1:]


def fold_kernel(place_ref, kept, received, out):
    second = pl.program_id(0)
    value = kept[place_ref[0], second].astype(F32) + received[0, 0].astype(F32)
    out[second] = value.astype(BF16)


def fold(place, kept, received):
    shape = kept.shape[1:]
    return pl.pallas_call(
        fold_kernel,
        grid_spec=pltpu.PrefetchScalarGridSpec(
            num_scalar_prefetch=1,
            grid=(shape[0],),
            in_specs=[
                IN_VMEM,
                pl.BlockSpec((1, 1, *shape[1:]), lambda second, place: (place[0], second, 0, 0, 0)),
            ],
            out_specs=IN_VMEM,
        ),
        out_shape=pltpu.VMEM(shape, BF16),
        compiler_params=pltpu.CompilerParams(vmem_limit_bytes=VMEM_LIMIT),
        name="fold",
    )(place.reshape(1).astype(jnp.int32), kept, in_hbm(received))


def after(array, *others):
    return lax.optimization_barrier((array, *others))[0]


class Stream:
    def __init__(self, lay, send, keep):
        core, x, high, low = lay.place()
        self.own, self.received = keep, [lay.swap_core(send)]
        self.stages = [
            (jnp.where(core == 0, x, low), lay.swap_first),
            (jnp.where(core == 0, low, x), lay.swap_second),
            (high, lay.swap_high),
        ]

    def step(self, *before):
        place, swap = self.stages.pop(0)
        received = self.received[0]
        if len(self.received) > 1:
            received = sum(array.astype(F32) for array in self.received)
        received = after(received, *before)
        if len(self.stages) == 2:
            count = received.shape[0]
            self.sent = [fold(place ^ step, self.own, received) for step in range(1, count)]
            self.own = fold(place, self.own, after(received, *self.sent))
        else:
            self.own, self.sent = spread(place, (self.own, received))
        self.received = [swap(array, step) for step, array in enumerate(self.sent, 1)]

    def pieces(self):
        return [self.own] + self.received


def gather_double(lay, array):
    array = array[None]
    for size, swap in ((lay.group, lay.swap_low), (lay.highs, lay.swap_high)):
        step = 1
        while step < size:
            array = jnp.concatenate([array, swap(array, step)])
            step *= 2
    return array


def sum_steps(lay, array):
    steps = []
    for size, swap in ((lay.group, lay.swap_low), (lay.highs, lay.swap_high)):
        step = 1
        while step < size:
            array = array + swap(array, step)
            steps.append(array)
            step *= 2
    return steps


def shards(
    images, warp_rows, warp_cols, tile_weight, tile_patch, match_rows, match_cols, src_row, src_col
):
    lay = Layout(images.shape[0], images.shape[1])
    tiles, side, patches = lay.tiles, lay.side, lay.patches
    core, x, high, low = lay.place()
    weight = tile_weight.astype(F32)

    warped, sends, keeps = warp(lay, tile_patch, tile_weight, images, warp_rows, warp_cols)
    streams = [Stream(lay, send, keep) for send, keep in zip(sends, keeps)]
    prepared = prepare(lay, src_row, src_col, match_rows[0], match_cols[0])
    for stream in streams:
        stream.step(*prepared)

    named = (tile_patch[:, None] == jnp.arange(patches)[None, :]).astype(F32)
    counts = jnp.sum(named.reshape(tiles // VIS_ROW, VIS_ROW, patches), axis=0)
    table = jnp.concatenate([counts, jnp.sum(named * weight[:, None], axis=0, keepdims=True)])
    table = jnp.pad(table, ((0, 7 - VIS_ROW), (0, 0))).T.reshape(1, -1)
    table = jnp.pad(table, ((0, 0), (0, side - table.shape[1])))
    sources = jnp.concatenate([src_row.astype(F32), src_col.astype(F32), table])
    sources = after(sources, streams[-1].sent[-1])
    gathered = gather_double(lay, sources)
    all_rows, all_cols = gathered[:, 0:1, :], gathered[:, 1:2, :]
    table = jnp.sum(gathered[:, 2:3, :], axis=0)
    tile_place = ((tile_patch // lay.group) ^ high) * lay.group + ((tile_patch % lay.group) ^ low)

    for stream in streams:
        stream.step(gathered)
    tile_place = after(tile_place, streams[-1].own)
    flux, sums = forced_flux(lay, tile_patch, tile_place, warped, all_rows, all_cols)
    for stream in streams:
        stream.step(sums)
    sums = after(sums, streams[-1].own)
    steps = sum_steps(lay, sums)
    sums = steps[-1].reshape(patches, VIS_ROW, side)

    extra = -(-(lay.visits + 1) // 8) * 8
    pieces = [piece for stream in streams for piece in stream.pieces()]
    pieces[0] = after(pieces[0], steps[0])
    messages, fluxes = match(lay, extra, pieces, prepared, table)
    parts = [messages[0]] + [lay.swap_visit(messages[step], step) for step in range(1, lay.visits)]
    fluxes = after(fluxes, steps[1])
    fluxes = lax.all_to_all(fluxes, AXES, 0, 0, tiled=True)
    coadd = coadd_rows(lay, match_cols[0], parts)
    zero, resid = finish(lay, tile_patch, table, flux, sums, fluxes)
    return (coadd[None], zero.reshape(-1), resid)


def solution(mesh):
    in_specs = (
        P(AXES, None, None),
        P(AXES, None, None),
        P(AXES, None, None),
        P(AXES),
        P(AXES),
        P("patch", None, None),
        P("patch", None, None),
        P("patch", None),
        P("patch", None),
    )
    out_specs = (P("patch", "visit", None), P("visit"), P(AXES, None))
    return jax.shard_map(shards, mesh=mesh, in_specs=in_specs, out_specs=out_specs, check_vma=False)
```

```python
import functools

import jax
import jax.numpy as jnp
from jax import lax
from jax.experimental import pallas as pl
from jax.experimental.pallas import tpu as pltpu
from jax.sharding import PartitionSpec as P

VIS_ROW = 4
CAP = 2
APERTURE = 2.5
HIGHEST = lax.Precision.HIGHEST
F32 = jnp.float32
BF16 = jnp.bfloat16
AXES = ("visit", "patch")
EXPONENT = -1.4426950408889634 / (2.0 * APERTURE * APERTURE)
VMEM_LIMIT = 20 * 1024 * 1024
WARP_LIMIT = 38 * 1024 * 1024
PARTS = 1
PAIR = 2
IN_VMEM = pl.BlockSpec(memory_space=pltpu.VMEM)
NT = (((1,), (1,)), ((), ()))
TN = (((0,), (0,)), ((), ()))


class Layout:
    def __init__(self, tiles, side):
        self.tiles, self.side = tiles, side
        self.visits, self.patches = lax.axis_size("visit"), lax.axis_size("patch")
        self.group = self.visits // 2
        self.highs = self.patches // self.group
        self.width = side // self.visits
        self.part = side // PARTS

    def place(self):
        visit, patch = lax.axis_index("visit"), lax.axis_index("patch")
        return visit % 2, visit // 2, patch // self.group, patch % self.group

    def permute(self, array, partner):
        pairs = []
        for visit in range(self.visits):
            for patch in range(self.patches):
                x, core, high, low = partner(visit // 2, visit % 2, patch // self.group, patch % self.group)
                target = (2 * x + core) * self.patches + self.group * high + low
                pairs.append((visit * self.patches + patch, target))
        return lax.ppermute(array, AXES, pairs)

    def swap_core(self, array):
        return self.permute(array, lambda x, core, high, low: (x, 1 - core, high, low))

    def swap_first(self, array, step):
        def partner(x, core, high, low):
            return (x ^ step, core, high, low) if core == 0 else (x, core, high, low ^ step)

        return self.permute(array, partner)

    def swap_second(self, array, step):
        def partner(x, core, high, low):
            return (x, core, high, low ^ step) if core == 0 else (x ^ step, core, high, low)

        return self.permute(array, partner)

    def swap_low(self, array, step):
        return self.permute(array, lambda x, core, high, low: (x, core, high, low ^ step))

    def swap_high(self, array, step):
        return self.permute(array, lambda x, core, high, low: (x, core, high ^ step, low))

    def swap_visit(self, array, step):
        def partner(x, core, high, low):
            visit = (2 * x + core) ^ step
            return visit // 2, visit % 2, high, low

        return self.permute(array, partner)


def warp_kernel(lay, patch_hbm, weight_hbm, images, rows, cols, warped, *refs):
    outs, refs = refs[: 2 * PARTS], refs[2 * PARTS :]
    image, row, col, half, result, weights, lines, stage, patches, named, chosen, arrive, leave, depart, small = refs
    sends, keeps = outs[:PARTS], outs[PARTS:]
    fetches = [
        pltpu.make_async_copy(patch_hbm, patches, small.at[0]),
        pltpu.make_async_copy(weight_hbm, weights, small.at[1]),
    ]
    for fetch in fetches:
        fetch.start()
    loads = []
    for tile in range(lay.tiles):
        loads.append(
            [
                pltpu.make_async_copy(source.at[tile], target.at[tile], arrive.at[kind, tile])
                for kind, (source, target) in enumerate(((images, image), (cols, col), (rows, row)))
            ]
        )
        for load in loads[-1]:
            load.start()
    stores = []
    for tile in range(lay.tiles + 1):
        if tile < lay.tiles:
            loads[tile][0].wait()
            loads[tile][1].wait()
        if tile:
            loads[tile - 1][2].wait()
        if tile == lay.tiles - 2:
            for patch in range(lay.patches):
                named[patch] = 0
                for slot in range(CAP):
                    chosen[patch, slot] = 0
            for fetch in fetches:
                fetch.wait()
            for other in range(lay.tiles):
                patch = patches[other]
                chosen[patch, named[patch]] = other
                named[patch] = named[patch] + 1
            spread = weights[...].astype(F32).reshape(1, lay.tiles)
            lane = lax.broadcasted_iota(jnp.int32, (1, lay.tiles), 1)
            for patch in range(lay.patches):
                for slot in range(CAP):
                    picked = jnp.logical_and(lane == chosen[patch, slot], named[patch] > slot)
                    weight = jnp.sum(jnp.where(picked, spread, 0.0), keepdims=True)
                    spot = patch * CAP + slot
                    lines[spot : spot + 1, :] = jnp.broadcast_to(weight, (1, lay.width))
        if tile < lay.tiles:
            half[tile % 2] = lax.dot_general(image[tile], col[tile], NT, preferred_element_type=F32).astype(BF16)
        if tile:
            last = tile - 1
            result[last] = jnp.dot(row[last], half[last % 2], preferred_element_type=F32).astype(BF16)
            stores.append(pltpu.make_async_copy(result.at[last], warped.at[last], leave.at[last]))
            stores[-1].start()

    def block(core, first, second, high):
        x, low = (first, second) if core == 0 else (second, first)
        start = (2 * x + core) * lay.width
        patch = high * lay.group + low
        value = 0.0
        for slot in range(CAP):
            tile = chosen[patch, slot]
            weight = lines[patch * CAP + slot : patch * CAP + slot + 1, :]
            value = value + weight * result[tile, :, start : start + lay.width].astype(F32)
        return value.astype(BF16)

    core = lax.axis_index("visit") % 2
    places = [(f, g, h) for f in range(lay.group) for g in range(lay.group) for h in range(lay.highs)]
    departures = [
        pltpu.make_async_copy(
            stage.at[first, second, high, pl.ds(part * lay.part, lay.part)],
            sends[part].at[first, second, high],
            depart.at[part, spot],
        )
        for part in range(PARTS)
        for spot, (first, second, high) in enumerate(places)
    ]
    for own in range(2):

        @pl.when(core == own)
        def _():
            for spot, (first, second, high) in enumerate(places):
                stage[first, second, high] = block(1 - own, first, second, high)
                for part in range(PARTS):
                    departures[part * len(places) + spot].start()
            for first, second, high in places:
                value = block(own, first, second, high)
                for part in range(PARTS):
                    keeps[part][first, second, high] = value[part * lay.part : (part + 1) * lay.part]

    for copy in stores + departures:
        copy.wait()


def in_hbm(array):
    return pltpu.with_memory_space_constraint(array, pltpu.HBM)


def warp(lay, tile_patch, weight, images, warp_rows, warp_cols):
    tiles, side = lay.tiles, lay.side
    pieces = (lay.group, lay.group, lay.highs, lay.part, lay.width)
    in_any = pl.BlockSpec(memory_space=pltpu.HBM)
    stack = pltpu.VMEM((tiles, side, side), BF16)
    out = pl.pallas_call(
        functools.partial(warp_kernel, lay),
        in_specs=[in_any] * 5,
        out_specs=[in_any] * (1 + PARTS) + [IN_VMEM] * PARTS,
        out_shape=[pltpu.HBM((tiles, side, side), BF16)]
        + [pltpu.HBM(pieces, BF16)] * PARTS
        + [pltpu.VMEM(pieces, BF16)] * PARTS,
        scratch_shapes=[
            stack,
            stack,
            stack,
            pltpu.VMEM((2, side, side), BF16),
            stack,
            pltpu.VMEM((tiles,), BF16),
            pltpu.VMEM((lay.patches * CAP, lay.width), F32),
            pltpu.VMEM((lay.group, lay.group, lay.highs, side, lay.width), BF16),
            pltpu.SMEM((tiles,), jnp.int32),
            pltpu.SMEM((lay.patches,), jnp.int32),
            pltpu.SMEM((lay.patches, CAP), jnp.int32),
            pltpu.SemaphoreType.DMA((3, tiles)),
            pltpu.SemaphoreType.DMA((tiles,)),
            pltpu.SemaphoreType.DMA((PARTS, lay.group * lay.group * lay.highs)),
            pltpu.SemaphoreType.DMA((2,)),
        ],
        compiler_params=pltpu.CompilerParams(vmem_limit_bytes=WARP_LIMIT),
        cost_estimate=pl.CostEstimate(
            flops=4 * tiles * side**3, bytes_accessed=8 * tiles * side * side, transcendentals=0
        ),
        name="warp",
    )(in_hbm(tile_patch), in_hbm(weight), in_hbm(images), in_hbm(warp_rows), in_hbm(warp_cols))
    return out[0], out[1 : 1 + PARTS], out[1 + PARTS :]


def profile(position, centers):
    distance = position - centers
    return jnp.exp2(distance * distance * EXPONENT).astype(BF16)


def flux_kernel(lay, patch_ref, place_ref, warped, *refs):
    step = pl.program_id(0)
    sources, (flux, sums) = refs[: 2 * PAIR], refs[2 * PAIR :]

    @pl.when(step == 0)
    def _():
        sums[...] = jnp.zeros_like(sums)

    position = lax.broadcasted_iota(jnp.int32, (lay.side, lay.side), 0).astype(F32)
    for local in range(PAIR):
        tile = step * PAIR + local
        row_prof = profile(position, sources[local][0])
        col_prof = profile(position, sources[PAIR + local][0])
        by_column = jnp.dot(warped[local], col_prof, preferred_element_type=F32)
        value = jnp.sum(by_column * row_prof.astype(F32), axis=0, keepdims=True)
        flux[tile] = value
        spot = patch_ref[tile] * VIS_ROW + tile % VIS_ROW
        sums[pl.ds(spot, 1), :] += value


def forced_flux(lay, tile_patch, tile_place, warped, src_row, src_col):
    tiles, side = lay.tiles, lay.side
    sources = [
        pl.BlockSpec((1, 1, side), lambda step, patch, place, local=local: (place[step * PAIR + local], 0, 0))
        for local in range(PAIR)
    ]
    return pl.pallas_call(
        functools.partial(flux_kernel, lay),
        grid_spec=pltpu.PrefetchScalarGridSpec(
            num_scalar_prefetch=2,
            grid=(tiles // PAIR,),
            in_specs=[pl.BlockSpec((PAIR, side, side), lambda step, *_: (step, 0, 0))] + sources * 2,
            out_specs=[IN_VMEM, IN_VMEM],
        ),
        out_shape=[
            jax.ShapeDtypeStruct((tiles, 1, side), F32),
            jax.ShapeDtypeStruct((VIS_ROW * lay.patches, side), F32),
        ],
        compiler_params=pltpu.CompilerParams(vmem_limit_bytes=VMEM_LIMIT),
        cost_estimate=pl.CostEstimate(
            flops=2 * tiles * side**3, bytes_accessed=2 * tiles * side * side, transcendentals=2 * tiles * side * side
        ),
        name="forced_flux",
    )(tile_patch, tile_place, in_hbm(warped), *([src_row] * PAIR + [src_col] * PAIR))


def split(array):
    upper = array.astype(BF16)
    return upper, (array - upper.astype(F32)).astype(BF16)


def dot3(left, right, dims):
    product = functools.partial(lax.dot_general, dimension_numbers=dims, preferred_element_type=F32)
    return product(left[0], right[0]) + (product(left[0], right[1]) + product(left[1], right[0]))


def prepare_kernel(lay, src_row, src_col, match_rows, match_cols, rows_up, rows_low, row_flux, col_up, col_low, product_ref):
    side = lay.side
    product = functools.partial(lax.dot_general, dimension_numbers=TN, preferred_element_type=F32)
    position = lax.broadcasted_iota(jnp.int32, (side, side), 0).astype(F32)
    row_prof = profile(position, src_row[...].astype(F32))
    col_prof = profile(position, src_col[...].astype(F32))
    upper, lower = split(match_rows[...])
    rows_up[...], rows_low[...] = upper, lower
    row_flux[...] = product(upper, row_prof) + product(lower, row_prof)
    upper, lower = split(match_cols[...])
    product_ref[...] = (product(upper, col_prof) + product(lower, col_prof)).reshape(lay.visits, lay.width, side)
    col_up[...], col_low[...] = split(product_ref[lax.axis_index("visit")])


def prepare(lay, src_row, src_col, match_rows, match_cols):
    side = lay.side
    block = pltpu.VMEM((lay.width, side), BF16)
    square = pltpu.VMEM((side, side), BF16)
    return pl.pallas_call(
        functools.partial(prepare_kernel, lay),
        in_specs=[IN_VMEM] * 4,
        out_specs=[IN_VMEM] * 5,
        out_shape=[square, square, pltpu.VMEM((side, side), F32), block, block],
        scratch_shapes=[pltpu.VMEM((lay.visits, lay.width, side), F32)],
        compiler_params=pltpu.CompilerParams(vmem_limit_bytes=VMEM_LIMIT),
        cost_estimate=pl.CostEstimate(
            flops=8 * side**3, bytes_accessed=20 * side * side, transcendentals=2 * side * side
        ),
        name="prepare",
    )(src_row, src_col, match_rows, match_cols)


def match_kernel(lay, extra, *refs):
    width, visits = lay.width, lay.visits
    pieces, refs = refs[: PARTS * lay.highs], refs[PARTS * lay.highs :]
    (rows_up, rows_low, row_flux, col_up, col_low, table), refs = refs[:6], refs[6:]
    messages, (spread, matched) = refs[:visits], refs[visits:]
    visit, patch = lax.axis_index("visit"), lax.axis_index("patch")
    stacked = jnp.concatenate(
        [
            sum(piece[...].astype(F32) for piece in pieces[part * lay.highs : (part + 1) * lay.highs])
            for part in range(PARTS)
        ],
        axis=0,
    )
    stacked = split(stacked)
    nn = (((1,), (0,)), ((), ()))
    result = dot3((rows_up[...], rows_low[...]), stacked, nn)
    matched[...] = result.reshape(visits, width, width)
    by_source = dot3(stacked, (col_up[...], col_low[...]), nn)
    flux = jnp.sum(by_source * row_flux[...], axis=0, keepdims=True)
    lane = lax.broadcasted_iota(jnp.int32, table.shape, 1)
    weight = jnp.sum(jnp.where(lane == patch * 8 + VIS_ROW, table[...], 0.0), keepdims=True)
    tail = jnp.concatenate(
        [flux[:, block * width : (block + 1) * width] for block in range(visits)]
        + [jnp.broadcast_to(weight, (extra - visits, width))],
        axis=0,
    )
    spread[...] = jnp.broadcast_to(tail[None], spread.shape)
    upper, lower = split(jnp.broadcast_to(weight, (8, width)))
    weight = jnp.concatenate([upper, lower], axis=0)
    for step, message in enumerate(messages):
        message[:width] = matched[visit ^ step].astype(BF16)
        message[width:] = weight


def match(lay, extra, pieces, prepared, table):
    side, width = lay.side, lay.width
    out = pl.pallas_call(
        functools.partial(match_kernel, lay, extra),
        in_specs=[IN_VMEM] * (len(pieces) + len(prepared) + 1),
        out_specs=[IN_VMEM] * (lay.visits + 1),
        out_shape=[pltpu.VMEM((width + 16, width), BF16)] * lay.visits
        + [jax.ShapeDtypeStruct((lay.visits * lay.patches, extra, width), F32)],
        scratch_shapes=[pltpu.VMEM((lay.visits, width, width), F32)],
        compiler_params=pltpu.CompilerParams(vmem_limit_bytes=VMEM_LIMIT),
        cost_estimate=pl.CostEstimate(
            flops=12 * width * side * side, bytes_accessed=10 * side * side, transcendentals=0
        ),
        name="match",
    )(*pieces, *prepared, table)
    return out[: lay.visits], out[lay.visits]


def coadd_kernel(lay, match_cols, *refs):
    parts, coadd = refs[:-1], refs[-1]
    width = lay.width
    visit = lax.axis_index("visit")
    blocks = []
    for block in range(lay.visits):
        value = parts[0][:width]
        for step in range(1, lay.visits):
            value = jnp.where((visit ^ step) == block, parts[step][:width], value)
        blocks.append(value)
    weight = 0.0
    for part in parts:
        halves = part[width:].astype(F32)
        weight = weight + (halves[0:1, 0:1] + halves[8:9, 0:1])
    blocks = jnp.concatenate(blocks, axis=1)
    product = functools.partial(lax.dot_general, dimension_numbers=NT, preferred_element_type=F32)
    upper, lower = split(match_cols[...])
    product = product(blocks, upper) + product(blocks, lower)
    coadd[...] = product / weight


def coadd_rows(lay, match_cols, parts):
    side, width = lay.side, lay.width
    return pl.pallas_call(
        functools.partial(coadd_kernel, lay),
        out_shape=jax.ShapeDtypeStruct((width, side), F32),
        compiler_params=pltpu.CompilerParams(vmem_limit_bytes=VMEM_LIMIT),
        cost_estimate=pl.CostEstimate(
            flops=12 * width * side * side, bytes_accessed=6 * side * side, transcendentals=0
        ),
        name="coadd_rows",
    )(match_cols, *parts)


def finish_kernel(lay, patch_ref, table, flux, sums, messages, zero, resid, lines):
    visits, patches = lay.visits, lay.patches
    for patch in range(patches):
        data = sum(messages[visit * patches + patch] for visit in range(visits))
        data = data / data[visits : visits + 1]
        lines[patch : patch + 1, :] = jnp.concatenate([data[block : block + 1] for block in range(visits)], axis=1)
    reference = lines[...]
    lane = lax.broadcasted_iota(jnp.int32, (patches, lay.side), 1) // 8
    row = lax.broadcasted_iota(jnp.int32, (patches, lay.side), 0)
    squares = jnp.sum(reference * reference, axis=1, keepdims=True)
    chosen = jnp.sum(jnp.where(lane == row, squares, 0.0), axis=0, keepdims=True) * table[...]
    products = 0.0
    denominators = 0.0
    for patch in range(patches):
        products = products + sums[patch] * reference[patch : patch + 1]
        denominators = denominators + chosen[:, patch * 8 : (patch + 1) * 8]
    columns = jnp.sum(products, axis=1, keepdims=True)
    place = lax.broadcasted_iota(jnp.int32, (1, VIS_ROW), 1)
    numerators = sum(jnp.where(place == visit, columns[visit : visit + 1], 0.0) for visit in range(VIS_ROW))
    scales = numerators / denominators[:, :VIS_ROW]
    zero[...] = scales
    for tile in range(lay.tiles):
        own = lines[pl.ds(patch_ref[tile], 1), :]
        visit = tile % VIS_ROW
        resid[tile : tile + 1, :] = flux[tile] - scales[:, visit : visit + 1] * own


def finish(lay, tile_patch, table, flux, sums, messages):
    return pl.pallas_call(
        functools.partial(finish_kernel, lay),
        in_specs=[pl.BlockSpec(memory_space=pltpu.SMEM)] + [IN_VMEM] * 4,
        out_specs=[IN_VMEM, IN_VMEM],
        out_shape=[
            jax.ShapeDtypeStruct((1, VIS_ROW), F32),
            jax.ShapeDtypeStruct((lay.tiles, lay.side), F32),
        ],
        scratch_shapes=[pltpu.VMEM((lay.patches, lay.side), F32)],
        compiler_params=pltpu.CompilerParams(vmem_limit_bytes=VMEM_LIMIT),
        name="finish",
    )(tile_patch, table, flux, sums, messages)


def spread_kernel(count, place_ref, kept, received, own, *sends):
    for step, out in enumerate((own, *sends)):
        spot = place_ref[0] ^ step
        out[...] = (kept[spot].astype(F32) + received[spot].astype(F32)).astype(out.dtype)


def spread(place, terms):
    kept, received = terms
    count, shape = kept.shape[0], kept.shape[1:]
    out = pl.pallas_call(
        functools.partial(spread_kernel, count),
        in_specs=[pl.BlockSpec(memory_space=pltpu.SMEM), IN_VMEM, IN_VMEM],
        out_specs=[IN_VMEM] * count,
        out_shape=[pltpu.VMEM(shape, BF16)] * count,
        compiler_params=pltpu.CompilerParams(vmem_limit_bytes=VMEM_LIMIT),
        name="spread",
    )(place.reshape(1).astype(jnp.int32), kept, received)
    return out[0], out[1:]


def fold_kernel(place_ref, kept, received, out):
    second = pl.program_id(0)
    value = kept[place_ref[0], second].astype(F32) + received[0, 0].astype(F32)
    out[second] = value.astype(BF16)


def fold(place, kept, received):
    shape = kept.shape[1:]
    return pl.pallas_call(
        fold_kernel,
        grid_spec=pltpu.PrefetchScalarGridSpec(
            num_scalar_prefetch=1,
            grid=(shape[0],),
            in_specs=[
                IN_VMEM,
                pl.BlockSpec((1, 1, *shape[1:]), lambda second, place: (place[0], second, 0, 0, 0)),
            ],
            out_specs=IN_VMEM,
        ),
        out_shape=pltpu.VMEM(shape, BF16),
        compiler_params=pltpu.CompilerParams(vmem_limit_bytes=VMEM_LIMIT),
        name="fold",
    )(place.reshape(1).astype(jnp.int32), kept, in_hbm(received))


def after(array, *others):
    return lax.optimization_barrier((array, *others))[0]


class Stream:
    def __init__(self, lay, send, keep):
        core, x, high, low = lay.place()
        self.own, self.received = keep, [lay.swap_core(send)]
        self.stages = [
            (jnp.where(core == 0, x, low), lay.swap_first),
            (jnp.where(core == 0, low, x), lay.swap_second),
            (high, lay.swap_high),
        ]

    def step(self, *before):
        place, swap = self.stages.pop(0)
        received = self.received[0]
        if len(self.received) > 1:
            received = sum(array.astype(F32) for array in self.received)
        received = after(received, *before)
        if len(self.stages) == 2:
            count = received.shape[0]
            self.sent = [fold(place ^ step, self.own, received) for step in range(1, count)]
            self.own = fold(place, self.own, after(received, *self.sent))
        else:
            self.own, self.sent = spread(place, (self.own, received))
        self.received = [swap(array, step) for step, array in enumerate(self.sent, 1)]

    def pieces(self):
        return [self.own] + self.received


def gather_patch(lay, near):
    return jnp.concatenate([near] + [lay.swap_high(near, step) for step in range(1, lay.highs)])


def sum_steps(lay, array):
    steps = []
    for size, swap in ((lay.group, lay.swap_low), (lay.highs, lay.swap_high)):
        step = 1
        while step < size:
            array = (array.astype(F32) + swap(array, step).astype(F32)).astype(array.dtype)
            steps.append(array)
            step *= 2
    return steps


def shards(
    images, warp_rows, warp_cols, tile_weight, tile_patch, match_rows, match_cols, src_row, src_col
):
    lay = Layout(images.shape[0], images.shape[1])
    tiles, side, patches = lay.tiles, lay.side, lay.patches
    core, x, high, low = lay.place()
    weight = tile_weight.astype(F32)

    warped, sends, keeps = warp(lay, tile_patch, tile_weight, images, warp_rows, warp_cols)
    named = (tile_patch[:, None] == jnp.arange(patches)[None, :]).astype(F32)
    counts = jnp.sum(named.reshape(tiles // VIS_ROW, VIS_ROW, patches), axis=0)
    table = jnp.concatenate([counts, jnp.sum(named * weight[:, None], axis=0, keepdims=True)])
    table = jnp.pad(table, ((0, 7 - VIS_ROW), (0, 0))).T.reshape(1, -1)
    table = jnp.pad(table, ((0, 0), (0, side - table.shape[1])))
    sources = jnp.concatenate([src_row.astype(F32), src_col.astype(F32), table])[None]
    sources = after(sources, keeps[-1])
    near = jnp.concatenate([sources] + [lay.swap_low(sources, step) for step in range(1, lay.group)])

    streams = [Stream(lay, send, keep) for send, keep in zip(sends, keeps)]
    for stream in streams:
        stream.step(near)
    gathered = gather_patch(lay, after(near, streams[-1].sent[-1]))
    all_rows, all_cols = gathered[:, 0:1, :], gathered[:, 1:2, :]
    table = jnp.sum(gathered[:, 2:3, :], axis=0)
    tile_place = ((tile_patch // lay.group) ^ high) * lay.group + ((tile_patch % lay.group) ^ low)
    flux, sums = forced_flux(lay, tile_patch, tile_place, warped, all_rows, all_cols)

    for stream in streams:
        stream.step(sums)
    steps = sum_steps(lay, after(sums.astype(BF16), streams[-1].own))
    prepared = prepare(lay, after(src_row, steps[1]), src_col, match_rows[0], match_cols[0])
    for stream in streams:
        stream.step(steps[1])

    extra = -(-(lay.visits + 1) // 8) * 8
    pieces = [piece for stream in streams for piece in stream.pieces()]
    messages, fluxes = match(lay, extra, pieces, prepared, table)
    parts = [messages[0]] + [lay.swap_visit(messages[step], step) for step in range(1, lay.visits)]
    fluxes = after(fluxes, steps[-1])
    fluxes = lax.all_to_all(fluxes, AXES, 0, 0, tiled=True)
    coadd = coadd_rows(lay, match_cols[0], parts)
    sums = steps[-1].astype(F32).reshape(patches, VIS_ROW, side)
    zero, resid = finish(lay, tile_patch, table, flux, sums, fluxes)
    return (coadd[None], zero.reshape(-1), resid)


def solution(mesh):
    in_specs = (
        P(AXES, None, None),
        P(AXES, None, None),
        P(AXES, None, None),
        P(AXES),
        P(AXES),
        P("patch", None, None),
        P("patch", None, None),
        P("patch", None),
        P("patch", None),
    )
    out_specs = (P("patch", "visit", None), P("visit"), P(AXES, None))
    return jax.shard_map(shards, mesh=mesh, in_specs=in_specs, out_specs=out_specs, check_vma=False)
```

```python
import functools

import jax
import jax.numpy as jnp
from jax import lax
from jax.experimental import pallas as pl
from jax.experimental.pallas import tpu as pltpu
from jax.sharding import PartitionSpec as P

VIS_ROW = 4
CAP = 2
APERTURE = 2.5
HIGHEST = lax.Precision.HIGHEST
F32 = jnp.float32
BF16 = jnp.bfloat16
AXES = ("visit", "patch")
EXPONENT = -1.4426950408889634 / (2.0 * APERTURE * APERTURE)
VMEM_LIMIT = 20 * 1024 * 1024
WARP_LIMIT = 38 * 1024 * 1024
PARTS = 1
PAIR = 2
IN_VMEM = pl.BlockSpec(memory_space=pltpu.VMEM)
NT = (((1,), (1,)), ((), ()))
NN = (((1,), (0,)), ((), ()))
TN = (((0,), (0,)), ((), ()))


class Layout:
    def __init__(self, tiles, side):
        self.tiles, self.side = tiles, side
        self.visits, self.patches = lax.axis_size("visit"), lax.axis_size("patch")
        self.group = self.visits // 2
        self.highs = self.patches // self.group
        self.width = side // self.visits
        self.part = side // PARTS

    def place(self):
        visit, patch = lax.axis_index("visit"), lax.axis_index("patch")
        return visit % 2, visit // 2, patch // self.group, patch % self.group

    def permute(self, array, partner):
        pairs = []
        for visit in range(self.visits):
            for patch in range(self.patches):
                x, core, high, low = partner(visit // 2, visit % 2, patch // self.group, patch % self.group)
                target = (2 * x + core) * self.patches + self.group * high + low
                pairs.append((visit * self.patches + patch, target))
        return lax.ppermute(array, AXES, pairs)

    def swap_core(self, array):
        return self.permute(array, lambda x, core, high, low: (x, 1 - core, high, low))

    def swap_first(self, array, step):
        def partner(x, core, high, low):
            return (x ^ step, core, high, low) if core == 0 else (x, core, high, low ^ step)

        return self.permute(array, partner)

    def swap_second(self, array, step):
        def partner(x, core, high, low):
            return (x, core, high, low ^ step) if core == 0 else (x ^ step, core, high, low)

        return self.permute(array, partner)

    def swap_low(self, array, step):
        return self.permute(array, lambda x, core, high, low: (x, core, high, low ^ step))

    def swap_high(self, array, step):
        return self.permute(array, lambda x, core, high, low: (x, core, high ^ step, low))

    def swap_visit(self, array, step):
        def partner(x, core, high, low):
            visit = (2 * x + core) ^ step
            return visit // 2, visit % 2, high, low

        return self.permute(array, partner)


def warp_kernel(lay, patch_hbm, weight_hbm, images, rows, cols, warped, *refs):
    outs, refs = refs[: 2 * PARTS], refs[2 * PARTS :]
    image, row, col, half, result, weights, lines, stage, patches, named, chosen, arrive, leave, depart, small = refs
    sends, keeps = outs[:PARTS], outs[PARTS:]
    fetches = [
        pltpu.make_async_copy(patch_hbm, patches, small.at[0]),
        pltpu.make_async_copy(weight_hbm, weights, small.at[1]),
    ]
    for fetch in fetches:
        fetch.start()
    loads = []
    for tile in range(lay.tiles):
        loads.append(
            [
                pltpu.make_async_copy(source.at[tile], target.at[tile], arrive.at[kind, tile])
                for kind, (source, target) in enumerate(((images, image), (cols, col), (rows, row)))
            ]
        )
        for load in loads[-1]:
            load.start()
    stores = []
    for tile in range(lay.tiles + 1):
        if tile < lay.tiles:
            loads[tile][0].wait()
            loads[tile][1].wait()
        if tile:
            loads[tile - 1][2].wait()
        if tile == lay.tiles - 2:
            for patch in range(lay.patches):
                named[patch] = 0
                for slot in range(CAP):
                    chosen[patch, slot] = 0
            for fetch in fetches:
                fetch.wait()
            for other in range(lay.tiles):
                patch = patches[other]
                chosen[patch, named[patch]] = other
                named[patch] = named[patch] + 1
            spread = weights[...].astype(F32).reshape(1, lay.tiles)
            lane = lax.broadcasted_iota(jnp.int32, (1, lay.tiles), 1)
            for patch in range(lay.patches):
                for slot in range(CAP):
                    picked = jnp.logical_and(lane == chosen[patch, slot], named[patch] > slot)
                    weight = jnp.sum(jnp.where(picked, spread, 0.0), keepdims=True)
                    spot = patch * CAP + slot
                    lines[spot : spot + 1, :] = jnp.broadcast_to(weight, (1, lay.width))
        if tile < lay.tiles:
            half[tile % 2] = lax.dot_general(image[tile], col[tile], NT, preferred_element_type=F32).astype(BF16)
        if tile:
            last = tile - 1
            result[last] = jnp.dot(row[last], half[last % 2], preferred_element_type=F32).astype(BF16)
            stores.append(pltpu.make_async_copy(result.at[last], warped.at[last], leave.at[last]))
            stores[-1].start()

    def block(core, first, second, high):
        x, low = (first, second) if core == 0 else (second, first)
        start = (2 * x + core) * lay.width
        patch = high * lay.group + low
        value = 0.0
        for slot in range(CAP):
            tile = chosen[patch, slot]
            weight = lines[patch * CAP + slot : patch * CAP + slot + 1, :]
            value = value + weight * result[tile, :, start : start + lay.width].astype(F32)
        return value.astype(BF16)

    core = lax.axis_index("visit") % 2
    places = [(f, g, h) for f in range(lay.group) for g in range(lay.group) for h in range(lay.highs)]
    departures = [
        pltpu.make_async_copy(
            stage.at[first, second, high, pl.ds(part * lay.part, lay.part)],
            sends[part].at[first, second, high],
            depart.at[part, spot],
        )
        for part in range(PARTS)
        for spot, (first, second, high) in enumerate(places)
    ]
    for own in range(2):

        @pl.when(core == own)
        def _():
            for spot, (first, second, high) in enumerate(places):
                stage[first, second, high] = block(1 - own, first, second, high)
                for part in range(PARTS):
                    departures[part * len(places) + spot].start()
            for first, second, high in places:
                value = block(own, first, second, high)
                for part in range(PARTS):
                    keeps[part][first, second, high] = value[part * lay.part : (part + 1) * lay.part]

    for copy in stores + departures:
        copy.wait()


def in_hbm(array):
    return pltpu.with_memory_space_constraint(array, pltpu.HBM)


def warp(lay, tile_patch, weight, images, warp_rows, warp_cols):
    tiles, side = lay.tiles, lay.side
    pieces = (lay.group, lay.group, lay.highs, lay.part, lay.width)
    in_any = pl.BlockSpec(memory_space=pltpu.HBM)
    stack = pltpu.VMEM((tiles, side, side), BF16)
    out = pl.pallas_call(
        functools.partial(warp_kernel, lay),
        in_specs=[in_any] * 5,
        out_specs=[in_any] * (1 + PARTS) + [IN_VMEM] * PARTS,
        out_shape=[pltpu.HBM((tiles, side, side), BF16)]
        + [pltpu.HBM(pieces, BF16)] * PARTS
        + [pltpu.VMEM(pieces, BF16)] * PARTS,
        scratch_shapes=[
            stack,
            stack,
            stack,
            pltpu.VMEM((2, side, side), BF16),
            stack,
            pltpu.VMEM((tiles,), BF16),
            pltpu.VMEM((lay.patches * CAP, lay.width), F32),
            pltpu.VMEM((lay.group, lay.group, lay.highs, side, lay.width), BF16),
            pltpu.SMEM((tiles,), jnp.int32),
            pltpu.SMEM((lay.patches,), jnp.int32),
            pltpu.SMEM((lay.patches, CAP), jnp.int32),
            pltpu.SemaphoreType.DMA((3, tiles)),
            pltpu.SemaphoreType.DMA((tiles,)),
            pltpu.SemaphoreType.DMA((PARTS, lay.group * lay.group * lay.highs)),
            pltpu.SemaphoreType.DMA((2,)),
        ],
        compiler_params=pltpu.CompilerParams(vmem_limit_bytes=WARP_LIMIT),
        cost_estimate=pl.CostEstimate(
            flops=4 * tiles * side**3, bytes_accessed=8 * tiles * side * side, transcendentals=0
        ),
        name="warp",
    )(in_hbm(tile_patch), in_hbm(weight), in_hbm(images), in_hbm(warp_rows), in_hbm(warp_cols))
    return out[0], out[1 : 1 + PARTS], out[1 + PARTS :]


def profile(position, centers):
    distance = position - centers
    return jnp.exp2(distance * distance * EXPONENT).astype(BF16)


def flux_kernel(lay, begin, patch_ref, place_ref, warped, *refs):
    step = pl.program_id(0)
    sources, (earlier, flux, sums) = refs[: 2 * PAIR], refs[2 * PAIR :]

    @pl.when(step == 0)
    def _():
        sums[...] = earlier[...]

    position = lax.broadcasted_iota(jnp.int32, (lay.side, lay.side), 0).astype(F32)
    for local in range(PAIR):
        tile = begin + step * PAIR + local
        row_prof = profile(position, sources[local][0])
        col_prof = profile(position, sources[PAIR + local][0])
        by_column = jnp.dot(warped[local], col_prof, preferred_element_type=F32)
        value = jnp.sum(by_column * row_prof.astype(F32), axis=0, keepdims=True)
        flux[step * PAIR + local] = value
        spot = patch_ref[tile] * VIS_ROW + tile % VIS_ROW
        sums[pl.ds(spot, 1), :] += value


def forced_flux(lay, begin, end, tile_patch, tile_place, warped, src_row, src_col, earlier):
    count, side = end - begin, lay.side
    sources = [
        pl.BlockSpec((1, 1, side), lambda step, patch, place, at=begin + local: (place[step * PAIR + at], 0, 0))
        for local in range(PAIR)
    ]
    return pl.pallas_call(
        functools.partial(flux_kernel, lay, begin),
        grid_spec=pltpu.PrefetchScalarGridSpec(
            num_scalar_prefetch=2,
            grid=(count // PAIR,),
            in_specs=[pl.BlockSpec((PAIR, side, side), lambda step, *_: (step + begin // PAIR, 0, 0))]
            + sources * 2
            + [IN_VMEM],
            out_specs=[IN_VMEM, IN_VMEM],
        ),
        out_shape=[
            jax.ShapeDtypeStruct((count, 1, side), F32),
            jax.ShapeDtypeStruct((VIS_ROW * lay.patches, side), F32),
        ],
        compiler_params=pltpu.CompilerParams(vmem_limit_bytes=VMEM_LIMIT),
        cost_estimate=pl.CostEstimate(
            flops=2 * count * side**3, bytes_accessed=2 * count * side * side, transcendentals=2 * count * side * side
        ),
        name="forced_flux",
    )(tile_patch, tile_place, in_hbm(warped), *([src_row] * PAIR + [src_col] * PAIR), earlier)


def split(array):
    upper = array.astype(BF16)
    return upper, (array - upper.astype(F32)).astype(BF16)


def dot3(left, right, dims):
    product = functools.partial(lax.dot_general, dimension_numbers=dims, preferred_element_type=F32)
    return product(left[0], right[0]) + (product(left[0], right[1]) + product(left[1], right[0]))


def prepare_kernel(lay, src_row, src_col, match_rows, match_cols, rows_up, rows_low, row_flux, col_up, col_low, product_ref):
    side = lay.side
    product = functools.partial(lax.dot_general, dimension_numbers=TN, preferred_element_type=F32)
    position = lax.broadcasted_iota(jnp.int32, (side, side), 0).astype(F32)
    row_prof = profile(position, src_row[...].astype(F32))
    col_prof = profile(position, src_col[...].astype(F32))
    upper, lower = split(match_rows[...])
    rows_up[...], rows_low[...] = upper, lower
    row_flux[...] = product(upper, row_prof) + product(lower, row_prof)
    upper, lower = split(match_cols[...])
    product_ref[...] = (product(upper, col_prof) + product(lower, col_prof)).reshape(lay.visits, lay.width, side)
    col_up[...], col_low[...] = split(product_ref[lax.axis_index("visit")])


def prepare(lay, src_row, src_col, match_rows, match_cols):
    side = lay.side
    block = pltpu.VMEM((lay.width, side), BF16)
    square = pltpu.VMEM((side, side), BF16)
    return pl.pallas_call(
        functools.partial(prepare_kernel, lay),
        in_specs=[IN_VMEM] * 4,
        out_specs=[IN_VMEM] * 5,
        out_shape=[square, square, pltpu.VMEM((side, side), F32), block, block],
        scratch_shapes=[pltpu.VMEM((lay.visits, lay.width, side), F32)],
        compiler_params=pltpu.CompilerParams(vmem_limit_bytes=VMEM_LIMIT),
        cost_estimate=pl.CostEstimate(
            flops=8 * side**3, bytes_accessed=20 * side * side, transcendentals=2 * side * side
        ),
        name="prepare",
    )(src_row, src_col, match_rows, match_cols)


def own_weight(lay, table):
    lane = lax.broadcasted_iota(jnp.int32, table.shape, 1)
    return jnp.sum(jnp.where(lane == lax.axis_index("patch") * 8 + VIS_ROW, table[...], 0.0), keepdims=True)


def stacked_columns(lay, pieces):
    parts = [
        sum(piece[...].astype(F32) for piece in pieces[part * lay.highs : (part + 1) * lay.highs])
        for part in range(PARTS)
    ]
    return split(jnp.concatenate(parts, axis=0))


def share_kernel(lay, extra, *refs):
    pieces, (row_flux, col_up, col_low, table, shares) = refs[:-5], refs[-5:]
    width, visits = lay.width, lay.visits
    stacked = stacked_columns(lay, pieces)
    by_source = dot3(stacked, (col_up[...], col_low[...]), NN)
    flux = jnp.sum(by_source * row_flux[...], axis=0, keepdims=True)
    tail = jnp.concatenate(
        [flux[:, block * width : (block + 1) * width] for block in range(visits)]
        + [jnp.broadcast_to(own_weight(lay, table), (extra - visits, width))],
        axis=0,
    )
    shares[...] = jnp.broadcast_to(tail[None], shares.shape)


def match_kernel(lay, *refs):
    width, visits = lay.width, lay.visits
    pieces, (rows_up, rows_low, table), refs = refs[: PARTS * lay.highs], refs[-visits - 4 : -visits - 1], refs[-visits - 1 :]
    messages, matched = refs[:-1], refs[-1]
    visit = lax.axis_index("visit")
    result = dot3((rows_up[...], rows_low[...]), stacked_columns(lay, pieces), NN)
    matched[...] = result.reshape(visits, width, width)
    upper, lower = split(jnp.broadcast_to(own_weight(lay, table), (8, width)))
    weight = jnp.concatenate([upper, lower], axis=0)
    for step, message in enumerate(messages):
        message[:width] = matched[visit ^ step].astype(BF16)
        message[width:] = weight


def match(lay, extra, pieces, prepared, table):
    side, width = lay.side, lay.width
    rows_up, rows_low, row_flux, col_up, col_low = prepared
    params = pltpu.CompilerParams(vmem_limit_bytes=VMEM_LIMIT)
    cost = pl.CostEstimate(flops=6 * width * side * side, bytes_accessed=5 * side * side, transcendentals=0)
    shares = pl.pallas_call(
        functools.partial(share_kernel, lay, extra),
        in_specs=[IN_VMEM] * (len(pieces) + 4),
        out_specs=IN_VMEM,
        out_shape=jax.ShapeDtypeStruct((lay.visits * lay.patches, extra, width), F32),
        compiler_params=params,
        cost_estimate=cost,
        name="share",
    )(*pieces, row_flux, col_up, col_low, table)
    messages = pl.pallas_call(
        functools.partial(match_kernel, lay),
        in_specs=[IN_VMEM] * (len(pieces) + 3),
        out_specs=[IN_VMEM] * lay.visits,
        out_shape=[pltpu.VMEM((width + 16, width), BF16)] * lay.visits,
        scratch_shapes=[pltpu.VMEM((lay.visits, width, width), F32)],
        compiler_params=params,
        cost_estimate=cost,
        name="match",
    )(*pieces, rows_up, rows_low, after(table, shares))
    return messages, shares


def coadd_kernel(lay, match_cols, *refs):
    parts, coadd = refs[:-1], refs[-1]
    width = lay.width
    visit = lax.axis_index("visit")
    blocks = []
    for block in range(lay.visits):
        value = parts[0][:width]
        for step in range(1, lay.visits):
            value = jnp.where((visit ^ step) == block, parts[step][:width], value)
        blocks.append(value)
    weight = 0.0
    for part in parts:
        halves = part[width:].astype(F32)
        weight = weight + (halves[0:1, 0:1] + halves[8:9, 0:1])
    blocks = jnp.concatenate(blocks, axis=1)
    product = functools.partial(lax.dot_general, dimension_numbers=NT, preferred_element_type=F32)
    upper, lower = split(match_cols[...])
    product = product(blocks, upper) + product(blocks, lower)
    coadd[...] = product / weight


def coadd_rows(lay, match_cols, parts):
    side, width = lay.side, lay.width
    return pl.pallas_call(
        functools.partial(coadd_kernel, lay),
        out_shape=jax.ShapeDtypeStruct((width, side), F32),
        compiler_params=pltpu.CompilerParams(vmem_limit_bytes=VMEM_LIMIT),
        cost_estimate=pl.CostEstimate(
            flops=12 * width * side * side, bytes_accessed=6 * side * side, transcendentals=0
        ),
        name="coadd_rows",
    )(match_cols, *parts)


def finish_kernel(lay, patch_ref, table, flux_a, flux_b, sums, messages, zero, resid, lines):
    visits, patches = lay.visits, lay.patches
    for patch in range(patches):
        data = sum(messages[visit * patches + patch] for visit in range(visits))
        data = data / data[visits : visits + 1]
        lines[patch : patch + 1, :] = jnp.concatenate([data[block : block + 1] for block in range(visits)], axis=1)
    reference = lines[...]
    lane = lax.broadcasted_iota(jnp.int32, (patches, lay.side), 1) // 8
    row = lax.broadcasted_iota(jnp.int32, (patches, lay.side), 0)
    squares = jnp.sum(reference * reference, axis=1, keepdims=True)
    chosen = jnp.sum(jnp.where(lane == row, squares, 0.0), axis=0, keepdims=True) * table[...]
    products = 0.0
    denominators = 0.0
    for patch in range(patches):
        products = products + sums[patch] * reference[patch : patch + 1]
        denominators = denominators + chosen[:, patch * 8 : (patch + 1) * 8]
    columns = jnp.sum(products, axis=1, keepdims=True)
    place = lax.broadcasted_iota(jnp.int32, (1, VIS_ROW), 1)
    numerators = sum(jnp.where(place == visit, columns[visit : visit + 1], 0.0) for visit in range(VIS_ROW))
    scales = numerators / denominators[:, :VIS_ROW]
    zero[...] = scales
    for tile in range(lay.tiles):
        own = lines[pl.ds(patch_ref[tile], 1), :]
        visit = tile % VIS_ROW
        flux = flux_a[tile] if tile < flux_a.shape[0] else flux_b[tile - flux_a.shape[0]]
        resid[tile : tile + 1, :] = flux - scales[:, visit : visit + 1] * own


def finish(lay, tile_patch, table, flux_a, flux_b, sums, messages):
    return pl.pallas_call(
        functools.partial(finish_kernel, lay),
        in_specs=[pl.BlockSpec(memory_space=pltpu.SMEM)] + [IN_VMEM] * 5,
        out_specs=[IN_VMEM, IN_VMEM],
        out_shape=[
            jax.ShapeDtypeStruct((1, VIS_ROW), F32),
            jax.ShapeDtypeStruct((lay.tiles, lay.side), F32),
        ],
        scratch_shapes=[pltpu.VMEM((lay.patches, lay.side), F32)],
        compiler_params=pltpu.CompilerParams(vmem_limit_bytes=VMEM_LIMIT),
        name="finish",
    )(tile_patch, table, flux_a, flux_b, sums, messages)


def spread_kernel(count, place_ref, kept, received, own, *sends):
    for step, out in enumerate((own, *sends)):
        spot = place_ref[0] ^ step
        out[...] = (kept[spot].astype(F32) + received[spot].astype(F32)).astype(out.dtype)


def spread(place, terms):
    kept, received = terms
    count, shape = kept.shape[0], kept.shape[1:]
    out = pl.pallas_call(
        functools.partial(spread_kernel, count),
        in_specs=[pl.BlockSpec(memory_space=pltpu.SMEM), IN_VMEM, IN_VMEM],
        out_specs=[IN_VMEM] * count,
        out_shape=[pltpu.VMEM(shape, BF16)] * count,
        compiler_params=pltpu.CompilerParams(vmem_limit_bytes=VMEM_LIMIT),
        name="spread",
    )(place.reshape(1).astype(jnp.int32), kept, received)
    return out[0], out[1:]


def fold_kernel(place_ref, kept, received, out):
    second = pl.program_id(0)
    value = kept[place_ref[0], second].astype(F32) + received[0, 0].astype(F32)
    out[second] = value.astype(BF16)


def fold(place, kept, received):
    shape = kept.shape[1:]
    return pl.pallas_call(
        fold_kernel,
        grid_spec=pltpu.PrefetchScalarGridSpec(
            num_scalar_prefetch=1,
            grid=(shape[0],),
            in_specs=[
                IN_VMEM,
                pl.BlockSpec((1, 1, *shape[1:]), lambda second, place: (place[0], second, 0, 0, 0)),
            ],
            out_specs=IN_VMEM,
        ),
        out_shape=pltpu.VMEM(shape, BF16),
        compiler_params=pltpu.CompilerParams(vmem_limit_bytes=VMEM_LIMIT),
        name="fold",
    )(place.reshape(1).astype(jnp.int32), kept, in_hbm(received))


def after(array, *others):
    return lax.optimization_barrier((array, *others))[0]


class Stream:
    def __init__(self, lay, send, keep):
        core, x, high, low = lay.place()
        self.own, self.received = keep, [lay.swap_core(send)]
        self.stages = [
            (jnp.where(core == 0, x, low), lay.swap_first),
            (jnp.where(core == 0, low, x), lay.swap_second),
            (high, lay.swap_high),
        ]

    def step(self, *before):
        place, swap = self.stages.pop(0)
        received = self.received[0]
        if len(self.received) > 1:
            received = sum(array.astype(F32) for array in self.received)
        received = after(received, *before)
        if len(self.stages) == 2:
            count = received.shape[0]
            self.sent = [fold(place ^ step, self.own, received) for step in range(1, count)]
            self.own = fold(place, self.own, after(received, *self.sent))
        else:
            self.own, self.sent = spread(place, (self.own, received))
        self.received = [swap(array, step) for step, array in enumerate(self.sent, 1)]

    def pieces(self):
        return [self.own] + self.received


def gather_patch(lay, near):
    return jnp.concatenate([near] + [lay.swap_high(near, step) for step in range(1, lay.highs)])


def add_wide(left, right):
    return (left.astype(F32) + right.astype(F32)).astype(left.dtype)


def swaps_of(swap, size):
    return [functools.partial(swap, step=1 << bit) for bit in range(size.bit_length() - 1)]


def shards(
    images, warp_rows, warp_cols, tile_weight, tile_patch, match_rows, match_cols, src_row, src_col
):
    lay = Layout(images.shape[0], images.shape[1])
    tiles, side, patches = lay.tiles, lay.side, lay.patches
    core, x, high, low = lay.place()
    weight = tile_weight.astype(F32)

    warped, sends, keeps = warp(lay, tile_patch, tile_weight, images, warp_rows, warp_cols)
    named = (tile_patch[:, None] == jnp.arange(patches)[None, :]).astype(F32)
    counts = jnp.sum(named.reshape(tiles // VIS_ROW, VIS_ROW, patches), axis=0)
    table = jnp.concatenate([counts, jnp.sum(named * weight[:, None], axis=0, keepdims=True)])
    table = jnp.pad(table, ((0, 7 - VIS_ROW), (0, 0))).T.reshape(1, -1)
    table = jnp.pad(table, ((0, 0), (0, side - table.shape[1])))
    sources = jnp.concatenate([src_row.astype(F32), src_col.astype(F32), table])[None]
    sources = after(sources, keeps[-1])
    near = jnp.concatenate([sources] + [lay.swap_low(sources, step) for step in range(1, lay.group)])

    streams = [Stream(lay, send, keep) for send, keep in zip(sends, keeps)]
    for stream in streams:
        stream.step(near)
    gathered = gather_patch(lay, after(near, streams[-1].sent[-1]))
    all_rows, all_cols = gathered[:, 0:1, :], gathered[:, 1:2, :]
    table = jnp.sum(gathered[:, 2:3, :], axis=0)
    tile_place = ((tile_patch // lay.group) ^ high) * lay.group + ((tile_patch % lay.group) ^ low)
    middle = tiles * 6 // 8 // PAIR * PAIR
    targets = (tile_patch, tile_place, warped, all_rows, all_cols)
    sums = jnp.zeros((VIS_ROW * patches, side), F32)
    flux_a, sums = forced_flux(lay, 0, middle, *targets, sums)

    for stream in streams:
        stream.step(sums)
    sums = after(sums, streams[-1].own)
    flux_b, sums = forced_flux(lay, middle, tiles, *targets, sums)
    sums = sums.astype(BF16)
    swaps = swaps_of(lay.swap_high, lay.highs) + swaps_of(lay.swap_low, lay.group)
    sums = add_wide(sums, swaps[0](sums))
    received = swaps[1](sums)
    for stream in streams:
        stream.step(sums)
    sums = add_wide(sums, after(received, streams[-1].own))
    for swap in swaps[2:]:
        sums = add_wide(sums, swap(sums))
    prepared = prepare(lay, after(src_row, streams[-1].own), src_col, match_rows[0], match_cols[0])

    extra = -(-(lay.visits + 1) // 8) * 8
    pieces = [piece for stream in streams for piece in stream.pieces()]
    messages, fluxes = match(lay, extra, pieces, prepared, table)
    parts = [messages[0]] + [lay.swap_visit(messages[step], step) for step in range(1, lay.visits)]
    fluxes = after(fluxes, sums)
    fluxes = lax.all_to_all(fluxes, AXES, 0, 0, tiled=True)
    coadd = coadd_rows(lay, match_cols[0], parts)
    sums = sums.astype(F32).reshape(patches, VIS_ROW, side)
    zero, resid = finish(lay, tile_patch, table, flux_a, flux_b, sums, fluxes)
    return (coadd[None], zero.reshape(-1), resid)


def solution(mesh):
    in_specs = (
        P(AXES, None, None),
        P(AXES, None, None),
        P(AXES, None, None),
        P(AXES),
        P(AXES),
        P("patch", None, None),
        P("patch", None, None),
        P("patch", None),
        P("patch", None),
    )
    out_specs = (P("patch", "visit", None), P("visit"), P(AXES, None))
    return jax.shard_map(shards, mesh=mesh, in_specs=in_specs, out_specs=out_specs, check_vma=False)
```

```python
import functools

import jax
import jax.numpy as jnp
from jax import lax
from jax.experimental import pallas as pl
from jax.experimental.pallas import tpu as pltpu
from jax.sharding import PartitionSpec as P

VIS_ROW = 4
CAP = 2
APERTURE = 2.5
HIGHEST = lax.Precision.HIGHEST
F32 = jnp.float32
BF16 = jnp.bfloat16
AXES = ("visit", "patch")
EXPONENT = -1.4426950408889634 / (2.0 * APERTURE * APERTURE)
VMEM_LIMIT = 20 * 1024 * 1024
WARP_LIMIT = 38 * 1024 * 1024
PARTS = 1
PAIR = 2
IN_VMEM = pl.BlockSpec(memory_space=pltpu.VMEM)
NT = (((1,), (1,)), ((), ()))
NN = (((1,), (0,)), ((), ()))
TN = (((0,), (0,)), ((), ()))


class Layout:
    def __init__(self, tiles, side):
        self.tiles, self.side = tiles, side
        self.visits, self.patches = lax.axis_size("visit"), lax.axis_size("patch")
        self.group = self.visits // 2
        self.highs = self.patches // self.group
        self.width = side // self.visits
        self.part = side // PARTS

    def place(self):
        visit, patch = lax.axis_index("visit"), lax.axis_index("patch")
        return visit % 2, visit // 2, patch // self.group, patch % self.group

    def permute(self, array, partner):
        pairs = []
        for visit in range(self.visits):
            for patch in range(self.patches):
                x, core, high, low = partner(visit // 2, visit % 2, patch // self.group, patch % self.group)
                target = (2 * x + core) * self.patches + self.group * high + low
                pairs.append((visit * self.patches + patch, target))
        return lax.ppermute(array, AXES, pairs)

    def swap_core(self, array):
        return self.permute(array, lambda x, core, high, low: (x, 1 - core, high, low))

    def swap_first(self, array, step):
        def partner(x, core, high, low):
            return (x ^ step, core, high, low) if core == 0 else (x, core, high, low ^ step)

        return self.permute(array, partner)

    def swap_second(self, array, step):
        def partner(x, core, high, low):
            return (x, core, high, low ^ step) if core == 0 else (x ^ step, core, high, low)

        return self.permute(array, partner)

    def swap_low(self, array, step):
        return self.permute(array, lambda x, core, high, low: (x, core, high, low ^ step))

    def swap_high(self, array, step):
        return self.permute(array, lambda x, core, high, low: (x, core, high ^ step, low))

    def swap_visit(self, array, step):
        def partner(x, core, high, low):
            visit = (2 * x + core) ^ step
            return visit // 2, visit % 2, high, low

        return self.permute(array, partner)


def warp_kernel(lay, patch_hbm, weight_hbm, images, rows, cols, warped, *refs):
    outs, refs = refs[: 2 * PARTS], refs[2 * PARTS :]
    image, row, col, half, result, weights, lines, stage, patches, named, chosen, arrive, leave, depart, small = refs
    sends, keeps = outs[:PARTS], outs[PARTS:]
    fetches = [
        pltpu.make_async_copy(patch_hbm, patches, small.at[0]),
        pltpu.make_async_copy(weight_hbm, weights, small.at[1]),
    ]
    for fetch in fetches:
        fetch.start()
    loads = []
    for tile in range(lay.tiles):
        loads.append(
            [
                pltpu.make_async_copy(source.at[tile], target.at[tile], arrive.at[kind, tile])
                for kind, (source, target) in enumerate(((images, image), (cols, col), (rows, row)))
            ]
        )
        for load in loads[-1]:
            load.start()
    stores = []
    for tile in range(lay.tiles + 1):
        if tile < lay.tiles:
            loads[tile][0].wait()
            loads[tile][1].wait()
        if tile:
            loads[tile - 1][2].wait()
        if tile == lay.tiles - 2:
            for patch in range(lay.patches):
                named[patch] = 0
                for slot in range(CAP):
                    chosen[patch, slot] = 0
            for fetch in fetches:
                fetch.wait()
            for other in range(lay.tiles):
                patch = patches[other]
                chosen[patch, named[patch]] = other
                named[patch] = named[patch] + 1
            spread = weights[...].astype(F32).reshape(1, lay.tiles)
            lane = lax.broadcasted_iota(jnp.int32, (1, lay.tiles), 1)
            for patch in range(lay.patches):
                for slot in range(CAP):
                    picked = jnp.logical_and(lane == chosen[patch, slot], named[patch] > slot)
                    weight = jnp.sum(jnp.where(picked, spread, 0.0), keepdims=True)
                    spot = patch * CAP + slot
                    lines[spot : spot + 1, :] = jnp.broadcast_to(weight, (1, lay.width))
        if tile < lay.tiles:
            half[tile % 2] = lax.dot_general(image[tile], col[tile], NT, preferred_element_type=F32).astype(BF16)
        if tile:
            last = tile - 1
            result[last] = jnp.dot(row[last], half[last % 2], preferred_element_type=F32).astype(BF16)
            stores.append(pltpu.make_async_copy(result.at[last], warped.at[last], leave.at[last]))
            stores[-1].start()

    def block(core, first, second, high):
        x, low = (first, second) if core == 0 else (second, first)
        start = (2 * x + core) * lay.width
        patch = high * lay.group + low
        value = 0.0
        for slot in range(CAP):
            tile = chosen[patch, slot]
            weight = lines[patch * CAP + slot : patch * CAP + slot + 1, :]
            value = value + weight * result[tile, :, start : start + lay.width].astype(F32)
        return value.astype(BF16)

    core = lax.axis_index("visit") % 2
    places = [(f, g, h) for f in range(lay.group) for g in range(lay.group) for h in range(lay.highs)]
    departures = [
        pltpu.make_async_copy(
            stage.at[first, second, high, pl.ds(part * lay.part, lay.part)],
            sends[part].at[first, second, high],
            depart.at[part, spot],
        )
        for part in range(PARTS)
        for spot, (first, second, high) in enumerate(places)
    ]
    for own in range(2):

        @pl.when(core == own)
        def _():
            for spot, (first, second, high) in enumerate(places):
                stage[first, second, high] = block(1 - own, first, second, high)
                for part in range(PARTS):
                    departures[part * len(places) + spot].start()
            for first, second, high in places:
                value = block(own, first, second, high)
                for part in range(PARTS):
                    keeps[part][first, second, high] = value[part * lay.part : (part + 1) * lay.part]

    for copy in stores + departures:
        copy.wait()


def in_hbm(array):
    return pltpu.with_memory_space_constraint(array, pltpu.HBM)


def warp(lay, tile_patch, weight, images, warp_rows, warp_cols):
    tiles, side = lay.tiles, lay.side
    pieces = (lay.group, lay.group, lay.highs, lay.part, lay.width)
    in_any = pl.BlockSpec(memory_space=pltpu.HBM)
    stack = pltpu.VMEM((tiles, side, side), BF16)
    out = pl.pallas_call(
        functools.partial(warp_kernel, lay),
        in_specs=[in_any] * 5,
        out_specs=[in_any] * (1 + PARTS) + [IN_VMEM] * PARTS,
        out_shape=[pltpu.HBM((tiles, side, side), BF16)]
        + [pltpu.HBM(pieces, BF16)] * PARTS
        + [pltpu.VMEM(pieces, BF16)] * PARTS,
        scratch_shapes=[
            stack,
            stack,
            stack,
            pltpu.VMEM((2, side, side), BF16),
            stack,
            pltpu.VMEM((tiles,), BF16),
            pltpu.VMEM((lay.patches * CAP, lay.width), F32),
            pltpu.VMEM((lay.group, lay.group, lay.highs, side, lay.width), BF16),
            pltpu.SMEM((tiles,), jnp.int32),
            pltpu.SMEM((lay.patches,), jnp.int32),
            pltpu.SMEM((lay.patches, CAP), jnp.int32),
            pltpu.SemaphoreType.DMA((3, tiles)),
            pltpu.SemaphoreType.DMA((tiles,)),
            pltpu.SemaphoreType.DMA((PARTS, lay.group * lay.group * lay.highs)),
            pltpu.SemaphoreType.DMA((2,)),
        ],
        compiler_params=pltpu.CompilerParams(vmem_limit_bytes=WARP_LIMIT),
        cost_estimate=pl.CostEstimate(
            flops=4 * tiles * side**3, bytes_accessed=8 * tiles * side * side, transcendentals=0
        ),
        name="warp",
    )(in_hbm(tile_patch), in_hbm(weight), in_hbm(images), in_hbm(warp_rows), in_hbm(warp_cols))
    return out[0], out[1 : 1 + PARTS], out[1 + PARTS :]


def profile(position, centers):
    distance = position - centers
    return jnp.exp2(distance * distance * EXPONENT).astype(BF16)


def flux_kernel(lay, begin, patch_ref, place_ref, warped, *refs):
    step = pl.program_id(0)
    sources, (earlier, flux, sums) = refs[: 2 * PAIR], refs[2 * PAIR :]

    @pl.when(step == 0)
    def _():
        sums[...] = earlier[...]

    position = lax.broadcasted_iota(jnp.int32, (lay.side, lay.side), 0).astype(F32)
    for local in range(PAIR):
        tile = begin + step * PAIR + local
        row_prof = profile(position, sources[local][0])
        col_prof = profile(position, sources[PAIR + local][0])
        by_column = jnp.dot(warped[local], col_prof, preferred_element_type=F32)
        value = jnp.sum(by_column * row_prof.astype(F32), axis=0, keepdims=True)
        flux[step * PAIR + local] = value
        spot = patch_ref[tile] * VIS_ROW + tile % VIS_ROW
        sums[pl.ds(spot, 1), :] += value


def forced_flux(lay, begin, end, tile_patch, tile_place, warped, src_row, src_col, earlier):
    count, side = end - begin, lay.side
    sources = [
        pl.BlockSpec((1, 1, side), lambda step, patch, place, at=begin + local: (place[step * PAIR + at], 0, 0))
        for local in range(PAIR)
    ]
    return pl.pallas_call(
        functools.partial(flux_kernel, lay, begin),
        grid_spec=pltpu.PrefetchScalarGridSpec(
            num_scalar_prefetch=2,
            grid=(count // PAIR,),
            in_specs=[pl.BlockSpec((PAIR, side, side), lambda step, *_: (step + begin // PAIR, 0, 0))]
            + sources * 2
            + [IN_VMEM],
            out_specs=[IN_VMEM, IN_VMEM],
        ),
        out_shape=[
            jax.ShapeDtypeStruct((count, 1, side), F32),
            jax.ShapeDtypeStruct((VIS_ROW * lay.patches, side), F32),
        ],
        compiler_params=pltpu.CompilerParams(vmem_limit_bytes=VMEM_LIMIT),
        cost_estimate=pl.CostEstimate(
            flops=2 * count * side**3, bytes_accessed=2 * count * side * side, transcendentals=2 * count * side * side
        ),
        name="forced_flux",
    )(tile_patch, tile_place, in_hbm(warped), *([src_row] * PAIR + [src_col] * PAIR), earlier)


def split(array):
    upper = array.astype(BF16)
    return upper, (array - upper.astype(F32)).astype(BF16)


def dot3(left, right, dims):
    product = functools.partial(lax.dot_general, dimension_numbers=dims, preferred_element_type=F32)
    return product(left[0], right[0]) + (product(left[0], right[1]) + product(left[1], right[0]))


def prepare_kernel(lay, src_row, src_col, match_rows, match_cols, rows_up, rows_low, row_flux, col_up, col_low, product_ref):
    side = lay.side
    product = functools.partial(lax.dot_general, dimension_numbers=TN, preferred_element_type=F32)
    position = lax.broadcasted_iota(jnp.int32, (side, side), 0).astype(F32)
    row_prof = profile(position, src_row[...].astype(F32))
    col_prof = profile(position, src_col[...].astype(F32))
    upper, lower = split(match_rows[...])
    rows_up[...], rows_low[...] = upper, lower
    row_flux[...] = product(upper, row_prof) + product(lower, row_prof)
    upper, lower = split(match_cols[...])
    product_ref[...] = (product(upper, col_prof) + product(lower, col_prof)).reshape(lay.visits, lay.width, side)
    col_up[...], col_low[...] = split(product_ref[lax.axis_index("visit")])


def prepare(lay, src_row, src_col, match_rows, match_cols):
    side = lay.side
    block = pltpu.VMEM((lay.width, side), BF16)
    square = pltpu.VMEM((side, side), BF16)
    return pl.pallas_call(
        functools.partial(prepare_kernel, lay),
        in_specs=[IN_VMEM] * 4,
        out_specs=[IN_VMEM] * 5,
        out_shape=[square, square, pltpu.VMEM((side, side), F32), block, block],
        scratch_shapes=[pltpu.VMEM((lay.visits, lay.width, side), F32)],
        compiler_params=pltpu.CompilerParams(vmem_limit_bytes=VMEM_LIMIT),
        cost_estimate=pl.CostEstimate(
            flops=8 * side**3, bytes_accessed=20 * side * side, transcendentals=2 * side * side
        ),
        name="prepare",
    )(src_row, src_col, match_rows, match_cols)


def own_weight(lay, table):
    lane = lax.broadcasted_iota(jnp.int32, table.shape, 1)
    return jnp.sum(jnp.where(lane == lax.axis_index("patch") * 8 + VIS_ROW, table[...], 0.0), keepdims=True)


def stacked_columns(lay, pieces):
    parts = [
        sum(piece[...].astype(F32) for piece in pieces[part * lay.highs : (part + 1) * lay.highs])
        for part in range(PARTS)
    ]
    return split(jnp.concatenate(parts, axis=0))


def share_kernel(lay, extra, *refs):
    pieces, (row_flux, col_up, col_low, table, shares) = refs[:-5], refs[-5:]
    width, visits = lay.width, lay.visits
    stacked = stacked_columns(lay, pieces)
    by_source = dot3(stacked, (col_up[...], col_low[...]), NN)
    flux = jnp.sum(by_source * row_flux[...], axis=0, keepdims=True)
    tail = jnp.concatenate(
        [flux[:, block * width : (block + 1) * width] for block in range(visits)]
        + [jnp.broadcast_to(own_weight(lay, table), (extra - visits, width))],
        axis=0,
    )
    shares[...] = jnp.broadcast_to(tail[None], shares.shape)


def match_kernel(lay, *refs):
    width, visits = lay.width, lay.visits
    pieces, (rows_up, rows_low, table), refs = refs[: PARTS * lay.highs], refs[-visits - 4 : -visits - 1], refs[-visits - 1 :]
    messages, matched = refs[:-1], refs[-1]
    visit = lax.axis_index("visit")
    result = dot3((rows_up[...], rows_low[...]), stacked_columns(lay, pieces), NN)
    matched[...] = result.reshape(visits, width, width)
    upper, lower = split(jnp.broadcast_to(own_weight(lay, table), (8, width)))
    weight = jnp.concatenate([upper, lower], axis=0)
    for step, message in enumerate(messages):
        message[:width] = matched[visit ^ step].astype(BF16)
        message[width:] = weight


def match(lay, extra, pieces, prepared, table):
    side, width = lay.side, lay.width
    rows_up, rows_low, row_flux, col_up, col_low = prepared
    params = pltpu.CompilerParams(vmem_limit_bytes=VMEM_LIMIT)
    cost = pl.CostEstimate(flops=6 * width * side * side, bytes_accessed=5 * side * side, transcendentals=0)
    shares = pl.pallas_call(
        functools.partial(share_kernel, lay, extra),
        in_specs=[IN_VMEM] * (len(pieces) + 4),
        out_specs=IN_VMEM,
        out_shape=jax.ShapeDtypeStruct((lay.visits * lay.patches, extra, width), F32),
        compiler_params=params,
        cost_estimate=cost,
        name="share",
    )(*pieces, row_flux, col_up, col_low, table)
    messages = pl.pallas_call(
        functools.partial(match_kernel, lay),
        in_specs=[IN_VMEM] * (len(pieces) + 3),
        out_specs=[IN_VMEM] * lay.visits,
        out_shape=[pltpu.VMEM((width + 16, width), BF16)] * lay.visits,
        scratch_shapes=[pltpu.VMEM((lay.visits, width, width), F32)],
        compiler_params=params,
        cost_estimate=cost,
        name="match",
    )(*pieces, rows_up, rows_low, after(table, shares))
    return messages, shares


def coadd_kernel(lay, match_cols, *refs):
    parts, coadd = refs[:-1], refs[-1]
    width = lay.width
    visit = lax.axis_index("visit")
    blocks = []
    for block in range(lay.visits):
        value = parts[0][:width]
        for step in range(1, lay.visits):
            value = jnp.where((visit ^ step) == block, parts[step][:width], value)
        blocks.append(value)
    weight = 0.0
    for part in parts:
        halves = part[width:].astype(F32)
        weight = weight + (halves[0:1, 0:1] + halves[8:9, 0:1])
    blocks = jnp.concatenate(blocks, axis=1)
    product = functools.partial(lax.dot_general, dimension_numbers=NT, preferred_element_type=F32)
    upper, lower = split(match_cols[...])
    product = product(blocks, upper) + product(blocks, lower)
    coadd[...] = product / weight


def coadd_rows(lay, match_cols, parts):
    side, width = lay.side, lay.width
    return pl.pallas_call(
        functools.partial(coadd_kernel, lay),
        out_shape=jax.ShapeDtypeStruct((width, side), F32),
        compiler_params=pltpu.CompilerParams(vmem_limit_bytes=VMEM_LIMIT),
        cost_estimate=pl.CostEstimate(
            flops=12 * width * side * side, bytes_accessed=6 * side * side, transcendentals=0
        ),
        name="coadd_rows",
    )(match_cols, *parts)


def finish_kernel(lay, patch_ref, table, flux_a, flux_b, sums, messages, zero, resid, lines):
    visits, patches = lay.visits, lay.patches
    for patch in range(patches):
        data = sum(messages[visit * patches + patch] for visit in range(visits))
        data = data / data[visits : visits + 1]
        lines[patch : patch + 1, :] = jnp.concatenate([data[block : block + 1] for block in range(visits)], axis=1)
    reference = lines[...]
    lane = lax.broadcasted_iota(jnp.int32, (patches, lay.side), 1) // 8
    row = lax.broadcasted_iota(jnp.int32, (patches, lay.side), 0)
    squares = jnp.sum(reference * reference, axis=1, keepdims=True)
    chosen = jnp.sum(jnp.where(lane == row, squares, 0.0), axis=0, keepdims=True) * table[...]
    products = 0.0
    denominators = 0.0
    for patch in range(patches):
        products = products + sums[patch] * reference[patch : patch + 1]
        denominators = denominators + chosen[:, patch * 8 : (patch + 1) * 8]
    columns = jnp.sum(products, axis=1, keepdims=True)
    place = lax.broadcasted_iota(jnp.int32, (1, VIS_ROW), 1)
    numerators = sum(jnp.where(place == visit, columns[visit : visit + 1], 0.0) for visit in range(VIS_ROW))
    scales = numerators / denominators[:, :VIS_ROW]
    zero[...] = scales
    for tile in range(lay.tiles):
        own = lines[pl.ds(patch_ref[tile], 1), :]
        visit = tile % VIS_ROW
        flux = flux_a[tile] if tile < flux_a.shape[0] else flux_b[tile - flux_a.shape[0]]
        resid[tile : tile + 1, :] = flux - scales[:, visit : visit + 1] * own


def finish(lay, tile_patch, table, flux_a, flux_b, sums, messages):
    return pl.pallas_call(
        functools.partial(finish_kernel, lay),
        in_specs=[pl.BlockSpec(memory_space=pltpu.SMEM)] + [IN_VMEM] * 5,
        out_specs=[IN_VMEM, IN_VMEM],
        out_shape=[
            jax.ShapeDtypeStruct((1, VIS_ROW), F32),
            jax.ShapeDtypeStruct((lay.tiles, lay.side), F32),
        ],
        scratch_shapes=[pltpu.VMEM((lay.patches, lay.side), F32)],
        compiler_params=pltpu.CompilerParams(vmem_limit_bytes=VMEM_LIMIT),
        name="finish",
    )(tile_patch, table, flux_a, flux_b, sums, messages)


def spread_kernel(count, place_ref, kept, received, own, *sends):
    for step, out in enumerate((own, *sends)):
        spot = place_ref[0] ^ step
        out[...] = (kept[spot].astype(F32) + received[spot].astype(F32)).astype(out.dtype)


def spread(place, terms):
    kept, received = terms
    count, shape = kept.shape[0], kept.shape[1:]
    out = pl.pallas_call(
        functools.partial(spread_kernel, count),
        in_specs=[pl.BlockSpec(memory_space=pltpu.SMEM), IN_VMEM, IN_VMEM],
        out_specs=[IN_VMEM] * count,
        out_shape=[pltpu.VMEM(shape, BF16)] * count,
        compiler_params=pltpu.CompilerParams(vmem_limit_bytes=VMEM_LIMIT),
        name="spread",
    )(place.reshape(1).astype(jnp.int32), kept, received)
    return out[0], out[1:]


def fold_kernel(place_ref, kept, received, out):
    second = pl.program_id(0)
    value = kept[place_ref[0], second].astype(F32) + received[0, 0].astype(F32)
    out[second] = value.astype(BF16)


def fold(place, kept, received):
    shape = kept.shape[1:]
    return pl.pallas_call(
        fold_kernel,
        grid_spec=pltpu.PrefetchScalarGridSpec(
            num_scalar_prefetch=1,
            grid=(shape[0],),
            in_specs=[
                IN_VMEM,
                pl.BlockSpec((1, 1, *shape[1:]), lambda second, place: (place[0], second, 0, 0, 0)),
            ],
            out_specs=IN_VMEM,
        ),
        out_shape=pltpu.VMEM(shape, BF16),
        compiler_params=pltpu.CompilerParams(vmem_limit_bytes=VMEM_LIMIT),
        name="fold",
    )(place.reshape(1).astype(jnp.int32), kept, in_hbm(received))


def after(array, *others):
    return lax.optimization_barrier((array, *others))[0]


class Stream:
    def __init__(self, lay, send, keep):
        core, x, high, low = lay.place()
        self.own, self.received = keep, [lay.swap_core(send)]
        self.stages = [
            (jnp.where(core == 0, x, low), lay.swap_first),
            (jnp.where(core == 0, low, x), lay.swap_second),
            (high, lay.swap_high),
        ]

    def step(self, *before):
        place, swap = self.stages.pop(0)
        received = self.received[0]
        if len(self.received) > 1:
            received = sum(array.astype(F32) for array in self.received)
        received = after(received, *before)
        if len(self.stages) == 2:
            count = received.shape[0]
            self.sent = [fold(place ^ step, self.own, received) for step in range(1, count)]
            self.own = fold(place, self.own, after(received, *self.sent))
        else:
            self.own, self.sent = spread(place, (self.own, received))
        order = sorted(range(1, len(self.sent) + 1), reverse=True)
        made = {step: swap(self.sent[step - 1], step) for step in order}
        self.received = [made[step] for step in sorted(made)]

    def pieces(self):
        return [self.own] + self.received


def gather_patch(lay, near):
    far = [lay.swap_high(near, step) for step in reversed(range(1, lay.highs))]
    return jnp.concatenate([near] + far[::-1])


def add_wide(left, right):
    return (left.astype(F32) + right.astype(F32)).astype(left.dtype)


def swaps_of(swap, size):
    return [functools.partial(swap, step=1 << bit) for bit in range(size.bit_length() - 1)]


def shards(
    images, warp_rows, warp_cols, tile_weight, tile_patch, match_rows, match_cols, src_row, src_col
):
    lay = Layout(images.shape[0], images.shape[1])
    tiles, side, patches = lay.tiles, lay.side, lay.patches
    core, x, high, low = lay.place()
    weight = tile_weight.astype(F32)

    warped, sends, keeps = warp(lay, tile_patch, tile_weight, images, warp_rows, warp_cols)
    named = (tile_patch[:, None] == jnp.arange(patches)[None, :]).astype(F32)
    counts = jnp.sum(named.reshape(tiles // VIS_ROW, VIS_ROW, patches), axis=0)
    table = jnp.concatenate([counts, jnp.sum(named * weight[:, None], axis=0, keepdims=True)])
    table = jnp.pad(table, ((0, 7 - VIS_ROW), (0, 0))).T.reshape(1, -1)
    table = jnp.pad(table, ((0, 0), (0, side - table.shape[1])))
    sources = jnp.concatenate([src_row.astype(F32), src_col.astype(F32), table])[None]
    sources = after(sources, keeps[-1])
    near = jnp.concatenate([sources] + [lay.swap_low(sources, step) for step in range(1, lay.group)])

    streams = [Stream(lay, send, keep) for send, keep in zip(sends, keeps)]
    for stream in streams:
        stream.step(near)
    gathered = gather_patch(lay, after(near, streams[-1].sent[-1]))
    all_rows, all_cols = gathered[:, 0:1, :], gathered[:, 1:2, :]
    table = jnp.sum(gathered[:, 2:3, :], axis=0)
    tile_place = ((tile_patch // lay.group) ^ high) * lay.group + ((tile_patch % lay.group) ^ low)
    middle = tiles * 6 // 8 // PAIR * PAIR
    targets = (tile_patch, tile_place, warped, all_rows, all_cols)
    sums = jnp.zeros((VIS_ROW * patches, side), F32)
    flux_a, sums = forced_flux(lay, 0, middle, *targets, sums)

    for stream in streams:
        stream.step(sums)
    sums = after(sums, streams[-1].own)
    flux_b, sums = forced_flux(lay, middle, tiles, *targets, sums)
    sums = sums.astype(BF16)
    swaps = swaps_of(lay.swap_high, lay.highs) + swaps_of(lay.swap_low, lay.group)
    sums = add_wide(sums, swaps[0](sums))
    received = swaps[1](sums)
    for stream in streams:
        stream.step(sums)
    sums = add_wide(sums, after(received, streams[-1].own))
    for swap in swaps[2:]:
        sums = add_wide(sums, swap(sums))
    prepared = prepare(lay, after(src_row, streams[-1].own), src_col, match_rows[0], match_cols[0])

    extra = -(-(lay.visits + 1) // 8) * 8
    pieces = [piece for stream in streams for piece in stream.pieces()]
    messages, fluxes = match(lay, extra, pieces, prepared, table)
    parts = [messages[0]] + [lay.swap_visit(messages[step], step) for step in range(1, lay.visits)]
    fluxes = after(fluxes, sums)
    fluxes = lax.all_to_all(fluxes, AXES, 0, 0, tiled=True)
    coadd = coadd_rows(lay, match_cols[0], parts)
    sums = sums.astype(F32).reshape(patches, VIS_ROW, side)
    zero, resid = finish(lay, tile_patch, table, flux_a, flux_b, sums, fluxes)
    return (coadd[None], zero.reshape(-1), resid)


def solution(mesh):
    in_specs = (
        P(AXES, None, None),
        P(AXES, None, None),
        P(AXES, None, None),
        P(AXES),
        P(AXES),
        P("patch", None, None),
        P("patch", None, None),
        P("patch", None),
        P("patch", None),
    )
    out_specs = (P("patch", "visit", None), P("visit"), P(AXES, None))
    return jax.shard_map(shards, mesh=mesh, in_specs=in_specs, out_specs=out_specs, check_vma=False)
```
